256 devices in a mesh: dp: 8 (over y, core), fsdp: 4 (over x), tensor: 8 (over z).
Axes of the slice: x: 4, y: 4, z: 8, core: 2. Of those that a mesh axis runs over, the one named last changes fastest.
Arguments:
- gradients: bfloat16 [8, 4096, 14336], P('dp', 'fsdp', 'tensor'), may hold values from -40 to 40
- errors: bfloat16 [8, 4096, 14336], P('dp', 'fsdp', 'tensor'), may hold values from -3 to 3
- start_factor: float32 [14336, 128], P('tensor'), may hold values from -6 to 6
Outputs:
- right_factor: float32 [14336, 128], P('tensor')
- new_errors: bfloat16 [8, 4096, 14336], P('dp', 'fsdp', 'tensor')
The draws below stay inside these ranges and needn't reach their ends.
All inputs are finite; a program needn't handle non-finite values.
Results may differ from the reference program's by a relative error of at most 0.0014.
Values sent between devices are 32-bit elements; how exact they have to be, the bound alone decides.
No kernel may reach another device: no remote copies, remote signals or barrier semaphores. Data moves between devices by JAX's collectives and lax.ppermute only.
A program may use at most 64 MiB of HBM per device.

```python
import jax
import jax.numpy as jnp
from jax import lax

D = 4096
FF = 14336
R = 128
REPLICAS = 8


def draw_gradients(key, part):
    key = jax.random.fold_in(key, 11)
    keys = jax.random.split(key, 3)
    row_scale = jnp.exp(jax.random.uniform(keys[0], (1, D, 1), jnp.float32, jnp.log(0.3), jnp.log(3.0)))
    col_scale = jnp.exp(jax.random.uniform(keys[1], (1, 1, FF), jnp.float32, jnp.log(0.5), jnp.log(5.0)))
    noise = jnp.clip(jax.random.normal(keys[2], (REPLICAS, D, FF), jnp.float32), -2.6, 2.6)
    return (noise * row_scale * col_scale).astype(jnp.bfloat16)


def draw_start_factor(key, part):
    key = jax.random.fold_in(key, 23)
    keys = jax.random.split(key, 5)
    order = jax.random.permutation(keys[0], R).astype(jnp.float32)
    depth = order * (2.3 / (R - 1))
    own_scale = jnp.power(10.0, -depth)[None, :]
    signs = (2 * jax.random.randint(keys[1], (R,), 0, 2) - 1).astype(jnp.float32)
    mixing = (jax.random.uniform(keys[2], (R,), jnp.float32, 0.5, 1.0) * signs)[None, :]
    common = jnp.clip(jax.random.normal(keys[3], (FF, 1), jnp.float32), -3.0, 3.0)
    own = jnp.clip(jax.random.normal(keys[4], (FF, R), jnp.float32), -3.0, 3.0)
    return (common * mixing + own * own_scale).astype(jnp.float32)


def level_of(key, shape, shards, smallest, largest):
    factor_of, own = 1.0, jax.random.fold_in(key, 6)
    for dim, blocks in shards:
        draws = jnp.exp(jax.random.uniform(jax.random.fold_in(own, dim), (blocks,), jnp.float32, smallest / len(shards), largest / len(shards)))
        factor_of = factor_of * jnp.repeat(draws, shape[dim] // blocks).reshape([-1 if axis == dim else 1 for axis in range(len(shape))])
    return factor_of


def normal_values(key, shape, scale, reach, cuts=(), held_as=jnp.bfloat16):
    array = jax.random.normal(key, shape, jnp.float32) * scale
    if len(cuts) > 0:
        array = level_of(key, shape, cuts, -0.22, 0.18) * array
    return jnp.clip(array, min=-reach, max=reach).astype(held_as)


def setup_inputs(seed: int = 0) -> dict:
    arg_keys = jax.random.split(jax.random.key(seed), 4)
    gradients = draw_gradients(jax.random.fold_in(arg_keys[3], 71), 0)
    errors = normal_values(arg_keys[1], (REPLICAS, D, FF), 0.5, 3.0, ((0, 8), (1, 4), (2, 8)))
    start_factor = draw_start_factor(jax.random.fold_in(arg_keys[3], 71), 0)
    return dict(gradients=gradients, errors=errors, start_factor=start_factor)


def orthonormal(sketch):
    for turn in range(2):
        gram_matrix = jnp.dot(sketch.T.astype(jnp.float32), sketch.astype(jnp.float32), precision=lax.Precision.HIGHEST, preferred_element_type=jnp.float32)
        lower_factor = jnp.linalg.cholesky(gram_matrix)
        sketch = lax.linalg.triangular_solve(lower_factor, sketch, left_side=False, lower=True, transpose_a=True)
    return sketch

def reference(gradients, errors, start_factor):

    def add_sketch(total, pair):
        merged = pair[0].astype(jnp.float32) + pair[1].astype(jnp.float32)
        return (total + jnp.dot(merged.astype(jnp.float32), start_factor.astype(jnp.float32), precision=lax.Precision.HIGHEST, preferred_element_type=jnp.float32), None)
    sketch, unused = lax.scan(add_sketch, jnp.zeros((D, R), jnp.float32), (gradients, errors))
    basis_cols = orthonormal(sketch)

    def add_factor(total, pair):
        merged = pair[0].astype(jnp.float32) + pair[1].astype(jnp.float32)
        term = lax.dot_general(merged.astype(jnp.float32), basis_cols.astype(jnp.float32), (((0,), (0,)), ((), ())), precision=lax.Precision.HIGHEST, preferred_element_type=jnp.float32)
        return (total + term, None)
    summed, unused = lax.scan(add_factor, jnp.zeros((FF, R), jnp.float32), (gradients, errors))
    right_factor = summed / REPLICAS

    def residue(pair):
        merged = pair[0].astype(jnp.float32) + pair[1].astype(jnp.float32)
        update = jnp.dot(basis_cols.astype(jnp.float32), right_factor.T.astype(jnp.float32), precision=lax.Precision.HIGHEST, preferred_element_type=jnp.float32)
        return (merged - update).astype(jnp.bfloat16)
    new_errors = lax.map(residue, (gradients, errors))
    return (right_factor, new_errors)
```

```python
import functools

import jax
import jax.numpy as jnp
from jax import lax
from jax.experimental import pallas as pl
from jax.experimental.pallas import tpu as pltpu
from jax.sharding import Mesh, PartitionSpec as P

F32, BF16 = jnp.float32, jnp.bfloat16
RANK = 128
ROWS = 256
COLS = 256
VMEM_LIMIT = 40 * 1024 * 1024
NT = (((1,), (1,)), ((), ()))
NN = (((1,), (0,)), ((), ()))
TN = (((0,), (0,)), ((), ()))


def mm(a, b, dims=NN):
    return lax.dot_general(a, b, dims, preferred_element_type=F32)


def mm32(a, b, dims=NN):
    return lax.dot_general(a, b, dims, precision=lax.Precision.HIGHEST, preferred_element_type=F32)


def split3(x):
    hi = x.astype(BF16)
    rest = x - hi.astype(F32)
    mid = rest.astype(BF16)
    low = (rest - mid.astype(F32)).astype(BF16)
    return hi, mid, low


def params():
    return pltpu.CompilerParams(vmem_limit_bytes=VMEM_LIMIT)


def sketch_kernel(g_ref, e_ref, p_ref, keep_ref, send_ref, p12, p3):
    step = pl.program_id(0)
    half_steps = pl.num_programs(0) // 2

    @pl.when(step == 0)
    def _():
        hi, mid, low = split3(p_ref[...])
        p12[:, :RANK] = hi
        p12[:, RANK:] = mid
        p3[...] = low

    g, e = g_ref[...], e_ref[...]
    both = mm(g, p12[...]) + mm(e, p12[...])
    block = both[:, :RANK] + both[:, RANK:] + mm(g + e, p3[...])
    mine = step // half_steps == lax.axis_index("core")
    rows = pl.ds(pl.multiple_of(lax.rem(step, half_steps) * ROWS, ROWS), ROWS)

    @pl.when(mine)
    def _():
        keep_ref[rows, :] = block

    @pl.when(jnp.logical_not(mine))
    def _():
        send_ref[rows, :] = block


def local_sketch(g, e, p):
    n, m = g.shape
    whole = pl.BlockSpec((n // 2, RANK), lambda i: (0, 0))
    out = jax.ShapeDtypeStruct((n // 2, RANK), F32)
    rows = min(ROWS, n // 2)
    return pl.pallas_call(
        sketch_kernel,
        grid=(n // rows,),
        in_specs=[
            pl.BlockSpec((rows, m), lambda i: (i, 0)),
            pl.BlockSpec((rows, m), lambda i: (i, 0)),
            pl.BlockSpec((m, RANK), lambda i: (0, 0)),
        ],
        out_specs=[whole, whole],
        out_shape=[out, out],
        scratch_shapes=[pltpu.VMEM((m, 2 * RANK), BF16), pltpu.VMEM((m, RANK), BF16)],
        compiler_params=params(),
        name="local_sketch",
    )(g, e, p)


def total_kernel(parts_ref, out_ref):
    total = parts_ref[0]
    for i in range(1, parts_ref.shape[0]):
        total = total + parts_ref[i]
    for i in range(parts_ref.shape[0]):
        out_ref[i] = total


def total_for_all(parts):
    return pl.pallas_call(
        total_kernel,
        out_shape=jax.ShapeDtypeStruct(parts.shape, F32),
        compiler_params=params(),
        name="sketch_total",
    )(parts)


def factor_kernel(own_ref, other_ref, g_ref, e_ref, sketch_ref, keep_ref, send_ref, gram_ref, s12, s3, turned):
    core = lax.axis_index("core")

    @pl.when(pl.program_id(0) == 0)
    def _():
        half = own_ref.shape[0]
        sketch_ref[pl.ds(pl.multiple_of(core * half, half), half), :] = own_ref[...]
        sketch_ref[pl.ds(pl.multiple_of((1 - core) * half, half), half), :] = other_ref[...]
        hi, mid, low = split3(sketch_ref[...].T)
        s12[:RANK, :] = hi
        s12[RANK:, :] = mid
        s3[...] = low
        square = mm(s12[...], s12[...], NT)
        cross = mm(s12[:RANK, :], s3[...], NT)
        gram_ref[...] = (
            square[:RANK, :RANK] + square[RANK:, RANK:]
            + (square[:RANK, RANK:] + square[RANK:, :RANK])
            + (cross + cross.T)
        )

    g, e = g_ref[...], e_ref[...]
    both = mm(s12[...], g) + mm(s12[...], e)
    block = both[:RANK] + both[RANK:] + mm(s3[...], g + e)
    turned[...] = block.T
    keep_ref[...] = turned[pl.ds(pl.multiple_of(core * RANK, RANK), RANK), :]
    send_ref[...] = turned[pl.ds(pl.multiple_of((1 - core) * RANK, RANK), RANK), :]


def factor_terms(own, other, g, e):
    n, m = g.shape
    half = pl.BlockSpec((n // 2, RANK), lambda j: (0, 0))
    block = pl.BlockSpec((n, COLS), lambda j: (0, j))
    rows = pl.BlockSpec((RANK, RANK), lambda j: (j, 0))
    return pl.pallas_call(
        factor_kernel,
        grid=(m // COLS,),
        in_specs=[half, half, block, block],
        out_specs=[
            pl.BlockSpec((n, RANK), lambda j: (0, 0)),
            rows,
            rows,
            pl.BlockSpec((RANK, RANK), lambda j: (0, 0)),
        ],
        out_shape=[
            jax.ShapeDtypeStruct((n, RANK), F32),
            jax.ShapeDtypeStruct((m // 2, RANK), F32),
            jax.ShapeDtypeStruct((m // 2, RANK), F32),
            jax.ShapeDtypeStruct((RANK, RANK), F32),
        ],
        scratch_shapes=[
            pltpu.VMEM((2 * RANK, n), BF16),
            pltpu.VMEM((RANK, n), BF16),
            pltpu.VMEM((COLS, RANK), F32),
        ],
        compiler_params=params(),
        name="factor_terms",
    )(own, other, g, e)


def pack_kernel(keep_ref, got_ref, gram_ref, out_ref):
    count, chunk = out_ref.shape[0], out_ref.shape[1]
    strip = RANK // lax.axis_size("y")
    piece = chunk - strip
    gram_rows = gram_ref[pl.ds(pl.multiple_of(lax.axis_index("y") * strip, strip), strip), :]
    for i in range(count):
        rows = pl.ds(i * piece, piece)
        out_ref[i, :piece] = keep_ref[rows, :] + got_ref[rows, :]
        out_ref[i, piece:] = gram_rows


def pack(keep, got, gram, count, strip):
    piece = keep.shape[0] // count
    return pl.pallas_call(
        pack_kernel,
        out_shape=jax.ShapeDtypeStruct((count, piece + strip, RANK), F32),
        compiler_params=params(),
        name="pack",
    )(keep, got, gram)


def gather_gram(parts_ref, gram_ref):
    strips, columns = lax.axis_size("y"), lax.axis_size("fsdp")
    strip = RANK // strips
    piece = parts_ref.shape[1] - strip
    for i in range(strips):
        total = parts_ref[i * columns, piece:]
        for k in range(1, columns):
            total = total + parts_ref[i * columns + k, piece:]
        gram_ref[i * strip : (i + 1) * strip, :] = total


def across(tile, lane):
    return jnp.broadcast_to(tile[:, lane : lane + 1], tile.shape)


def down(tile, row):
    return jnp.broadcast_to(tile[row : row + 1, :], tile.shape)


def invert_cholesky(a_ref, b_ref, out_ref):
    tiles = RANK // 8
    lane = lax.broadcasted_iota(jnp.int32, (8, RANK), 1)
    row = lax.broadcasted_iota(jnp.int32, (8, RANK), 0)
    for t in range(tiles):
        b_ref[8 * t : 8 * t + 8, :] = jnp.where(lane == row + 8 * t, 1.0, 0.0)
    for t in range(tiles):
        here = slice(8 * t, 8 * t + 8)
        a_tile, b_tile = a_ref[here, :], b_ref[here, :]
        columns = [across(a_tile, 8 * t + k) for k in range(8)]
        value = {(i, k): down(columns[k], i) for k in range(8) for i in range(k, 8)}
        factor, inverse, root = {}, [], []
        for k in range(8):
            inverse.append(1.0 / value[k, k])
            root.append(lax.rsqrt(value[k, k]))
            for i in range(k + 1, 8):
                factor[i, k] = value[i, k] * inverse[k]
            for j in range(k + 1, 8):
                for i in range(j, 8):
                    value[i, j] = value[i, j] - factor[j, k] * value[i, k]
        a_rows = [down(a_tile, k) for k in range(8)]
        b_rows = [down(b_tile, k) for k in range(8)]
        for k in range(8):
            for i in range(k + 1, 8):
                a_rows[i] = a_rows[i] - factor[i, k] * a_rows[k]
                b_rows[i] = b_rows[i] - factor[i, k] * b_rows[k]
        for k in range(8):
            out_ref[8 * t + k : 8 * t + k + 1, :] = (b_rows[k] * root[k])[:1, :]
        for u in range(t + 1, tiles):
            there = slice(8 * u, 8 * u + 8)
            a_low, b_low = a_ref[there, :], b_ref[there, :]
            left = [across(a_low, 8 * t + k) for k in range(8)]
            for k in range(8):
                for i in range(k + 1, 8):
                    left[i] = left[i] - factor[i, k] * left[k]
                scaled = left[k] * inverse[k]
                a_low = a_low - scaled * a_rows[k]
                b_low = b_low - scaled * b_rows[k]
            a_ref[there, :] = a_low
            b_ref[there, :] = b_low


def first_pass_kernel(parts_ref, sketch_ref, basis_ref, inv_ref, out_ref, a_ref, b_ref, gram_ref):
    strip = RANK // lax.axis_size("y")
    count, chunk = parts_ref.shape[0], parts_ref.shape[1]
    piece = chunk - strip
    gather_gram(parts_ref, a_ref)
    invert_cholesky(a_ref, b_ref, inv_ref)
    basis = mm32(sketch_ref[...], inv_ref[...], NT)
    basis_ref[...] = basis
    gram_ref[...] = mm32(basis, basis, TN)
    total = parts_ref[0, :piece]
    for i in range(1, count):
        total = total + parts_ref[i, :piece]
    gram_rows = gram_ref[pl.ds(pl.multiple_of(lax.axis_index("y") * strip, strip), strip), :]
    for i in range(count):
        out_ref[i, :piece] = total
        out_ref[i, piece:] = gram_rows


def first_pass(parts, sketch):
    square = jax.ShapeDtypeStruct((RANK, RANK), F32)
    return pl.pallas_call(
        first_pass_kernel,
        out_shape=[
            jax.ShapeDtypeStruct(sketch.shape, F32),
            square,
            jax.ShapeDtypeStruct(parts.shape, F32),
        ],
        scratch_shapes=[pltpu.VMEM((RANK, RANK), F32)] * 3,
        compiler_params=params(),
        name="first_pass",
    )(parts, sketch)


def second_pass_kernel(parts_ref, basis_one_ref, inv_one_ref, basis_ref, inv_ref, a_ref, b_ref, two_ref):
    gather_gram(parts_ref, a_ref)
    invert_cholesky(a_ref, b_ref, two_ref)
    basis_ref[...] = mm32(basis_one_ref[...], two_ref[...], NT)
    inv_ref[...] = mm32(two_ref[...], inv_one_ref[...])


def second_pass(parts, basis_one, inv_one):
    return pl.pallas_call(
        second_pass_kernel,
        out_shape=[
            jax.ShapeDtypeStruct(basis_one.shape, F32),
            jax.ShapeDtypeStruct(inv_one.shape, F32),
        ],
        scratch_shapes=[pltpu.VMEM((RANK, RANK), F32)] * 3,
        compiler_params=params(),
        name="second_pass",
    )(parts, basis_one, inv_one)


def residue_kernel(replicas, own_ref, other_ref, basis_ref, inv_ref, g_ref, e_ref, right_ref, new_ref, halves, q12):
    step = pl.program_id(0)

    @pl.when(step == 0)
    def _():
        core = lax.axis_index("core")
        strip = RANK // lax.axis_size("y")
        count, chunk = own_ref.shape[0], own_ref.shape[1]
        piece = chunk - strip
        for i in range(count):
            halves[core, i * piece : (i + 1) * piece, :] = own_ref[i, :piece]
            halves[1 - core, i * piece : (i + 1) * piece, :] = other_ref[i, :piece]
        basis = basis_ref[...]
        hi = basis.astype(BF16)
        q12[:, :RANK] = hi
        q12[:, RANK:] = (basis - hi.astype(F32)).astype(BF16)

    rows = pl.ds(pl.multiple_of(step * RANK, RANK), RANK)
    raw = jnp.concatenate([halves[0, rows, :], halves[1, rows, :]], axis=0)
    right = mm32(raw, inv_ref[...], NT) * (1.0 / replicas)
    right_ref[...] = right
    hi = right.astype(BF16)
    low = (right - hi.astype(F32)).astype(BF16)
    update = mm(q12[...], jnp.concatenate([hi, hi], axis=1), NT) + mm(q12[:, :RANK], low, NT)
    new_ref[...] = (g_ref[...].astype(F32) + e_ref[...].astype(F32) - update).astype(BF16)


def residue(own, other, basis, inv, g, e, replicas):
    n, m = g.shape
    parts = pl.BlockSpec(own.shape, lambda j: (0, 0, 0))
    block = pl.BlockSpec((n, COLS), lambda j: (0, j))
    return pl.pallas_call(
        functools.partial(residue_kernel, replicas),
        grid=(m // COLS,),
        in_specs=[
            parts,
            parts,
            pl.BlockSpec((n, RANK), lambda j: (0, 0)),
            pl.BlockSpec((RANK, RANK), lambda j: (0, 0)),
            block,
            block,
        ],
        out_specs=[pl.BlockSpec((COLS, RANK), lambda j: (j, 0)), block],
        out_shape=[jax.ShapeDtypeStruct((m, RANK), F32), jax.ShapeDtypeStruct((n, m), BF16)],
        scratch_shapes=[
            pltpu.VMEM((2, m // 2, RANK), F32),
            pltpu.VMEM((n, 2 * RANK), BF16),
        ],
        compiler_params=params(),
        name="residue",
    )(own, other, basis, inv, g, e)


def swap(x):
    return lax.ppermute(x, "core", [(0, 1), (1, 0)])


def shards(gradients, errors, start_factor):
    g, e = gradients[0], errors[0]
    n = g.shape[0]
    ny, nx, nz = lax.axis_size("y"), lax.axis_size("fsdp"), lax.axis_size("tensor")
    keep, send = local_sketch(g, e, start_factor)
    pieces = (keep + swap(send)).reshape(ny * nz, -1, RANK)
    pieces = lax.all_to_all(pieces, ("y", "tensor"), 0, 0)
    own = lax.all_to_all(total_for_all(pieces), ("y", "tensor"), 0, 0).reshape(n // 2, RANK)
    sketch, keep, send, gram = factor_terms(own, swap(own), g, e)
    parts = pack(keep, swap(send), gram, ny * nx, RANK // ny)
    parts = lax.all_to_all(parts, ("y", "fsdp"), 0, 0)
    basis_one, inv_one, parts = first_pass(parts, sketch)
    parts = lax.all_to_all(parts, ("y", "fsdp"), 0, 0)
    other = swap(parts)
    basis, inv = second_pass(parts, basis_one, inv_one)
    right_factor, new_errors = residue(parts, other, basis, inv, g, e, 2 * ny)
    return (right_factor, new_errors[None])


def solution(mesh):
    shape = mesh.devices.shape
    split = Mesh(
        mesh.devices.reshape(shape[0] // 2, 2, *shape[1:]), ("y", "core", "fsdp", "tensor")
    )
    big = P(("y", "core"), "fsdp", "tensor")
    return jax.shard_map(
        shards,
        mesh=split,
        in_specs=(big, big, P("tensor", None)),
        out_specs=(P("tensor", None), big),
        check_vma=False,
    )
```

```python
import functools

import jax
import jax.numpy as jnp
from jax import lax
from jax.experimental import pallas as pl
from jax.experimental.pallas import tpu as pltpu
from jax.sharding import Mesh, PartitionSpec as P

F32, BF16 = jnp.float32, jnp.bfloat16
RANK = 128
ROWS = 256
COLS = 256
VMEM_LIMIT = 24 * 1024 * 1024
STREAM_LIMIT = 55500000
NT = (((1,), (1,)), ((), ()))
NN = (((1,), (0,)), ((), ()))
TN = (((0,), (0,)), ((), ()))


def mm(a, b, dims=NN):
    return lax.dot_general(a, b, dims, preferred_element_type=F32)


def mm32(a, b, dims=NN):
    return lax.dot_general(a, b, dims, precision=lax.Precision.HIGHEST, preferred_element_type=F32)


def split3(x):
    hi = x.astype(BF16)
    rest = x - hi.astype(F32)
    mid = rest.astype(BF16)
    low = (rest - mid.astype(F32)).astype(BF16)
    return hi, mid, low


def params(limit=VMEM_LIMIT):
    return pltpu.CompilerParams(vmem_limit_bytes=limit)


def sketch_kernel(g_hbm, e_hbm, p_hbm, keep_ref, send_ref, g_ref, e_ref, p_ref, p12, p3, sems):
    n = g_ref.shape[0]
    steps, ahead = n // ROWS, 2
    core = lax.axis_index("core")

    def load(i):
        rows = pl.ds(i * ROWS, ROWS)
        return (
            pltpu.make_async_copy(g_hbm.at[rows], g_ref.at[rows], sems.at[2 * i]),
            pltpu.make_async_copy(e_hbm.at[rows], e_ref.at[rows], sems.at[2 * i + 1]),
        )

    first = pltpu.make_async_copy(p_hbm, p_ref, sems.at[2 * steps])
    first.start()
    copies = [load(i) for i in range(steps)]
    for i in range(ahead):
        copies[i][0].start()
        copies[i][1].start()
    first.wait()
    hi, mid, low = split3(p_ref[...])
    p12[:, :RANK] = hi
    p12[:, RANK:] = mid
    p3[...] = low
    for i in range(steps):
        copies[i][0].wait()
        copies[i][1].wait()
        if i + ahead < steps:
            copies[i + ahead][0].start()
            copies[i + ahead][1].start()
        rows = pl.ds(i * ROWS, ROWS)
        g, e = g_ref[rows, :], e_ref[rows, :]
        both = mm(g, p12[...]) + mm(e, p12[...])
        block = both[:, :RANK] + both[:, RANK:] + mm(g + e, p3[...])
        half = i // (steps // 2)
        place = pl.ds((i - half * (steps // 2)) * ROWS, ROWS)

        @pl.when(core == half)
        def _():
            keep_ref[place, :] = block

        @pl.when(core != half)
        def _():
            send_ref[place, :] = block


def local_sketch(g, e, p):
    n, m = g.shape
    half = jax.ShapeDtypeStruct((n // 2, RANK), F32)
    return pl.pallas_call(
        sketch_kernel,
        in_specs=[pl.BlockSpec(memory_space=pltpu.HBM)] * 3,
        out_specs=[pl.BlockSpec(memory_space=pltpu.VMEM)] * 2,
        out_shape=[half, half],
        scratch_shapes=[
            pltpu.VMEM((n, m), BF16),
            pltpu.VMEM((n, m), BF16),
            pltpu.VMEM((m, RANK), F32),
            pltpu.VMEM((m, 2 * RANK), BF16),
            pltpu.VMEM((m, RANK), BF16),
            pltpu.SemaphoreType.DMA((2 * (n // ROWS) + 1,)),
        ],
        compiler_params=params(STREAM_LIMIT),
        name="local_sketch",
    )(g, e, p)


def total_kernel(parts_ref, out_ref):
    total = parts_ref[0]
    for i in range(1, parts_ref.shape[0]):
        total = total + parts_ref[i]
    for i in range(parts_ref.shape[0]):
        out_ref[i] = total


def total_for_all(parts):
    return pl.pallas_call(
        total_kernel,
        out_shape=jax.ShapeDtypeStruct(parts.shape, F32),
        compiler_params=params(),
        cost_estimate=pl.CostEstimate(flops=2 * 10**10, bytes_accessed=5 * 10**7, transcendentals=0),
        name="sketch_total",
    )(parts)


def factor_block(s12, s3, g_ref, e_ref, out_ref, side):
    width = out_ref.shape[0]
    for start in range(0, width, COLS):
        size = min(COLS, width - start)
        cols = pl.ds(pl.multiple_of(side * width + start, RANK), size)
        g, e = g_ref[:, cols], e_ref[:, cols]
        both = mm(s12, g) + mm(s12, e)
        out_ref[start : start + size, :] = (both[:RANK] + both[RANK:] + mm(s3, g + e)).T


def factor_send_kernel(own_ref, other_ref, g_ref, e_ref, sketch_ref, s12_ref, s3_ref, gram_ref, send_ref):
    core = lax.axis_index("core")
    half = own_ref.shape[0]
    sketch_ref[pl.ds(pl.multiple_of(core * half, half), half), :] = own_ref[...]
    sketch_ref[pl.ds(pl.multiple_of((1 - core) * half, half), half), :] = other_ref[...]
    hi, mid, low = split3(sketch_ref[...].T)
    s12_ref[:RANK, :] = hi
    s12_ref[RANK:, :] = mid
    s3_ref[...] = low
    square = mm(s12_ref[...], s12_ref[...], NT)
    cross = mm(hi, low, NT)
    gram_ref[...] = (
        square[:RANK, :RANK] + square[RANK:, RANK:]
        + (square[:RANK, RANK:] + square[RANK:, :RANK])
        + (cross + cross.T)
    )
    factor_block(s12_ref[...], s3_ref[...], g_ref, e_ref, send_ref, 1 - core)


def factor_keep_kernel(s12_ref, s3_ref, g_ref, e_ref, keep_ref):
    factor_block(s12_ref[...], s3_ref[...], g_ref, e_ref, keep_ref, lax.axis_index("core"))


def factor_send(own, other, g, e):
    n, m = g.shape
    return pl.pallas_call(
        factor_send_kernel,
        out_shape=[
            jax.ShapeDtypeStruct((n, RANK), F32),
            jax.ShapeDtypeStruct((2 * RANK, n), BF16),
            jax.ShapeDtypeStruct((RANK, n), BF16),
            jax.ShapeDtypeStruct((RANK, RANK), F32),
            jax.ShapeDtypeStruct((m // 2, RANK), F32),
        ],
        compiler_params=params(),
        name="factor_send",
    )(own, other, g, e)


def factor_keep(s12, s3, g, e):
    return pl.pallas_call(
        factor_keep_kernel,
        out_shape=jax.ShapeDtypeStruct((g.shape[1] // 2, RANK), F32),
        compiler_params=params(),
        cost_estimate=pl.CostEstimate(flops=10**9, bytes_accessed=8 * 10**6, transcendentals=0),
        name="factor_keep",
    )(s12, s3, g, e)


def pack_kernel(keep_ref, got_ref, gram_ref, out_ref):
    count, chunk = out_ref.shape[0], out_ref.shape[1]
    strip = RANK // lax.axis_size("y")
    piece = chunk - strip
    gram_rows = gram_ref[pl.ds(pl.multiple_of(lax.axis_index("y") * strip, strip), strip), :]
    for i in range(count):
        rows = pl.ds(i * piece, piece)
        out_ref[i, :piece] = keep_ref[rows, :] + got_ref[rows, :]
        out_ref[i, piece:] = gram_rows


def pack(keep, got, gram, count, strip):
    piece = keep.shape[0] // count
    return pl.pallas_call(
        pack_kernel,
        out_shape=jax.ShapeDtypeStruct((count, piece + strip, RANK), F32),
        compiler_params=params(),
        name="pack",
    )(keep, got, gram)


def gather_gram(parts_ref, gram_ref):
    strips, columns = lax.axis_size("y"), lax.axis_size("fsdp")
    strip = RANK // strips
    piece = parts_ref.shape[1] - strip
    for i in range(strips):
        total = parts_ref[i * columns, piece:]
        for k in range(1, columns):
            total = total + parts_ref[i * columns + k, piece:]
        gram_ref[i * strip : (i + 1) * strip, :] = total


def across(tile, lane):
    return jnp.broadcast_to(tile[:, lane : lane + 1], tile.shape)


def down(tile, row):
    return jnp.broadcast_to(tile[row : row + 1, :], tile.shape)


def invert_cholesky(a_ref, b_ref, out_ref):
    tiles = RANK // 8
    lane = lax.broadcasted_iota(jnp.int32, (8, RANK), 1)
    row = lax.broadcasted_iota(jnp.int32, (8, RANK), 0)
    for t in range(tiles):
        b_ref[8 * t : 8 * t + 8, :] = jnp.where(lane == row + 8 * t, 1.0, 0.0)
    for t in range(tiles):
        here = slice(8 * t, 8 * t + 8)
        a_tile, b_tile = a_ref[here, :], b_ref[here, :]
        columns = [across(a_tile, 8 * t + k) for k in range(8)]
        value = {(i, k): down(columns[k], i) for k in range(8) for i in range(k, 8)}
        factor, inverse, root = {}, [], []
        for k in range(8):
            inverse.append(1.0 / value[k, k])
            root.append(lax.rsqrt(value[k, k]))
            for i in range(k + 1, 8):
                factor[i, k] = value[i, k] * inverse[k]
            for j in range(k + 1, 8):
                for i in range(j, 8):
                    value[i, j] = value[i, j] - factor[j, k] * value[i, k]
        a_rows = [down(a_tile, k) for k in range(8)]
        b_rows = [down(b_tile, k) for k in range(8)]
        for k in range(8):
            for i in range(k + 1, 8):
                a_rows[i] = a_rows[i] - factor[i, k] * a_rows[k]
                b_rows[i] = b_rows[i] - factor[i, k] * b_rows[k]
        for k in range(8):
            out_ref[8 * t + k : 8 * t + k + 1, :] = (b_rows[k] * root[k])[:1, :]
        for u in range(t + 1, tiles):
            there = slice(8 * u, 8 * u + 8)
            a_low, b_low = a_ref[there, :], b_ref[there, :]
            left = [across(a_low, 8 * t + k) for k in range(8)]
            for k in range(8):
                for i in range(k + 1, 8):
                    left[i] = left[i] - factor[i, k] * left[k]
                scaled = left[k] * inverse[k]
                a_low = a_low - scaled * a_rows[k]
                b_low = b_low - scaled * b_rows[k]
            a_ref[there, :] = a_low
            b_ref[there, :] = b_low


def first_pass_kernel(parts_ref, sketch_ref, basis_ref, inv_ref, out_ref, a_ref, b_ref, gram_ref):
    strip = RANK // lax.axis_size("y")
    count, chunk = parts_ref.shape[0], parts_ref.shape[1]
    piece = chunk - strip
    gather_gram(parts_ref, a_ref)
    invert_cholesky(a_ref, b_ref, inv_ref)
    basis = mm32(sketch_ref[...], inv_ref[...], NT)
    basis_ref[...] = basis
    gram_ref[...] = mm32(basis, basis, TN)
    total = parts_ref[0, :piece]
    for i in range(1, count):
        total = total + parts_ref[i, :piece]
    gram_rows = gram_ref[pl.ds(pl.multiple_of(lax.axis_index("y") * strip, strip), strip), :]
    for i in range(count):
        out_ref[i, :piece] = total
        out_ref[i, piece:] = gram_rows


def first_pass(parts, sketch):
    square = jax.ShapeDtypeStruct((RANK, RANK), F32)
    return pl.pallas_call(
        first_pass_kernel,
        out_shape=[
            jax.ShapeDtypeStruct(sketch.shape, F32),
            square,
            jax.ShapeDtypeStruct(parts.shape, F32),
        ],
        scratch_shapes=[pltpu.VMEM((RANK, RANK), F32)] * 3,
        compiler_params=params(),
        name="first_pass",
    )(parts, sketch)


def second_pass_kernel(parts_ref, basis_one_ref, inv_one_ref, basis_ref, inv_ref, a_ref, b_ref, two_ref):
    gather_gram(parts_ref, a_ref)
    invert_cholesky(a_ref, b_ref, two_ref)
    basis_ref[...] = mm32(basis_one_ref[...], two_ref[...], NT)
    inv_ref[...] = mm32(two_ref[...], inv_one_ref[...])


def second_pass(parts, basis_one, inv_one):
    return pl.pallas_call(
        second_pass_kernel,
        out_shape=[
            jax.ShapeDtypeStruct(basis_one.shape, F32),
            jax.ShapeDtypeStruct(inv_one.shape, F32),
        ],
        scratch_shapes=[pltpu.VMEM((RANK, RANK), F32)] * 3,
        compiler_params=params(),
        name="second_pass",
    )(parts, basis_one, inv_one)


def residue_kernel(replicas, own_ref, other_ref, basis_ref, inv_ref, g_ref, e_ref, right_hbm, new_hbm, halves, q12, right_ref, new_ref, sems):
    core = lax.axis_index("core")
    strip = RANK // lax.axis_size("y")
    count, chunk = own_ref.shape[0], own_ref.shape[1]
    piece = chunk - strip
    m = g_ref.shape[1]
    for i in range(count):
        halves[pl.ds(pl.multiple_of(core * (m // 2), 8) + i * piece, piece), :] = own_ref[i, :piece]
        halves[pl.ds(pl.multiple_of((1 - core) * (m // 2), 8) + i * piece, piece), :] = other_ref[i, :piece]
    basis = basis_ref[...]
    hi = basis.astype(BF16)
    q12[:, :RANK] = hi
    q12[:, RANK:] = (basis - hi.astype(F32)).astype(BF16)
    steps = m // COLS
    copies = []
    for j in range(steps):
        cols = pl.ds(j * COLS, COLS)
        right = mm32(halves[cols, :], inv_ref[...], NT) * (1.0 / replicas)
        right_ref[cols, :] = right
        hi = right.astype(BF16)
        low = (right - hi.astype(F32)).astype(BF16)
        update = mm(q12[...], jnp.concatenate([hi, hi], axis=1), NT) + mm(q12[:, :RANK], low, NT)
        new_ref[:, cols] = (g_ref[:, cols].astype(F32) + e_ref[:, cols].astype(F32) - update).astype(BF16)
        copies.append(pltpu.make_async_copy(right_ref.at[cols], right_hbm.at[cols], sems.at[2 * j]))
        copies.append(pltpu.make_async_copy(new_ref.at[:, cols], new_hbm.at[:, cols], sems.at[2 * j + 1]))
        copies[-2].start()
        copies[-1].start()
    for copy in copies:
        copy.wait()


def residue(own, other, basis, inv, g, e, replicas):
    n, m = g.shape
    return pl.pallas_call(
        functools.partial(residue_kernel, replicas),
        in_specs=[pl.BlockSpec(memory_space=pltpu.VMEM)] * 6,
        out_specs=[pl.BlockSpec(memory_space=pltpu.HBM)] * 2,
        out_shape=[jax.ShapeDtypeStruct((m, RANK), F32), jax.ShapeDtypeStruct((n, m), BF16)],
        scratch_shapes=[
            pltpu.VMEM((m, RANK), F32),
            pltpu.VMEM((n, 2 * RANK), BF16),
            pltpu.VMEM((m, RANK), F32),
            pltpu.VMEM((n, m), BF16),
            pltpu.SemaphoreType.DMA((2 * (m // COLS),)),
        ],
        compiler_params=params(),
        name="residue",
    )(own, other, basis, inv, g, e)


def swap(x):
    return lax.ppermute(x, "core", [(0, 1), (1, 0)])


def shards(gradients, errors, start_factor):
    g, e = gradients[0], errors[0]
    n = g.shape[0]
    ny, nx, nz = lax.axis_size("y"), lax.axis_size("fsdp"), lax.axis_size("tensor")
    keep, send = local_sketch(g, e, start_factor)
    pieces = (keep + swap(send)).reshape(ny * nz, -1, RANK)
    pieces = lax.all_to_all(pieces, ("y", "tensor"), 0, 0)
    own = lax.all_to_all(total_for_all(pieces), ("y", "tensor"), 0, 0).reshape(n // 2, RANK)
    sketch, s12, s3, gram, send = factor_send(own, swap(own), g, e)
    got = swap(send)
    parts = pack(factor_keep(s12, s3, g, e), got, gram, ny * nx, RANK // ny)
    parts = lax.all_to_all(parts, ("y", "fsdp"), 0, 0)
    basis_one, inv_one, parts = first_pass(parts, sketch)
    parts = lax.all_to_all(parts, ("y", "fsdp"), 0, 0)
    other = swap(parts)
    basis, inv = second_pass(parts, basis_one, inv_one)
    right_factor, new_errors = residue(parts, other, basis, inv, g, e, 2 * ny)
    return (right_factor, new_errors[None])


def solution(mesh):
    shape = mesh.devices.shape
    split = Mesh(
        mesh.devices.reshape(shape[0] // 2, 2, *shape[1:]), ("y", "core", "fsdp", "tensor")
    )
    big = P(("y", "core"), "fsdp", "tensor")
    return jax.shard_map(
        shards,
        mesh=split,
        in_specs=(big, big, P("tensor", None)),
        out_specs=(P("tensor", None), big),
        check_vma=False,
    )
```

```python
import functools

import jax
import jax.numpy as jnp
from jax import lax
from jax.experimental import pallas as pl
from jax.experimental.pallas import tpu as pltpu
from jax.sharding import Mesh, PartitionSpec as P

F32, BF16 = jnp.float32, jnp.bfloat16
RANK = 128
ROWS = 256
COLS = 256
VMEM_LIMIT = 24 * 1024 * 1024
TOP = 512
FETCH_LIMIT = 51000000
RESIDUE_LIMIT = 51000000
STREAM_LIMIT = 55500000
NT = (((1,), (1,)), ((), ()))
NN = (((1,), (0,)), ((), ()))
TN = (((0,), (0,)), ((), ()))


def mm(a, b, dims=NN):
    return lax.dot_general(a, b, dims, preferred_element_type=F32)


def mm32(a, b, dims=NN):
    return lax.dot_general(a, b, dims, precision=lax.Precision.HIGHEST, preferred_element_type=F32)


def split3(x):
    hi = x.astype(BF16)
    rest = x - hi.astype(F32)
    mid = rest.astype(BF16)
    low = (rest - mid.astype(F32)).astype(BF16)
    return hi, mid, low


VMEM_SPEC = pl.BlockSpec(memory_space=pltpu.VMEM)
HBM_SPEC = pl.BlockSpec(memory_space=pltpu.HBM)


def params(limit=VMEM_LIMIT):
    return pltpu.CompilerParams(vmem_limit_bytes=limit)


def sketch_kernel(g_hbm, e_hbm, p_hbm, keep_ref, send_ref, g_ref, e_ref, p_ref, p12, p3, sems):
    n = g_ref.shape[0]
    steps, ahead = n // ROWS, 2
    core = lax.axis_index("core")

    def load(i):
        rows = pl.ds(i * ROWS, ROWS)
        return (
            pltpu.make_async_copy(g_hbm.at[rows], g_ref.at[rows], sems.at[2 * i]),
            pltpu.make_async_copy(e_hbm.at[rows], e_ref.at[rows], sems.at[2 * i + 1]),
        )

    first = pltpu.make_async_copy(p_hbm, p_ref, sems.at[2 * steps])
    first.start()
    copies = [load(i) for i in range(steps)]
    for i in range(ahead):
        copies[i][0].start()
        copies[i][1].start()
    first.wait()
    hi, mid, low = split3(p_ref[...])
    p12[:, :RANK] = hi
    p12[:, RANK:] = mid
    p3[...] = low
    for i in range(steps):
        copies[i][0].wait()
        copies[i][1].wait()
        if i + ahead < steps:
            copies[i + ahead][0].start()
            copies[i + ahead][1].start()
        rows = pl.ds(i * ROWS, ROWS)
        g, e = g_ref[rows, :], e_ref[rows, :]
        both = mm(g, p12[...]) + mm(e, p12[...])
        block = both[:, :RANK] + both[:, RANK:] + mm(g + e, p3[...])
        half = i // (steps // 2)
        place = pl.ds((i - half * (steps // 2)) * ROWS, ROWS)

        @pl.when(core == half)
        def _():
            keep_ref[place, :] = block

        @pl.when(core != half)
        def _():
            send_ref[place, :] = block


def local_sketch(g, e, p):
    n, m = g.shape
    half = jax.ShapeDtypeStruct((n // 2, RANK), F32)
    return pl.pallas_call(
        sketch_kernel,
        in_specs=[HBM_SPEC] * 3,
        out_specs=[VMEM_SPEC] * 2,
        out_shape=[half, half],
        scratch_shapes=[
            pltpu.VMEM((n, m), BF16),
            pltpu.VMEM((n, m), BF16),
            pltpu.VMEM((m, RANK), F32),
            pltpu.VMEM((m, 2 * RANK), BF16),
            pltpu.VMEM((m, RANK), BF16),
            pltpu.SemaphoreType.DMA((2 * (n // ROWS) + 1,)),
        ],
        compiler_params=params(STREAM_LIMIT),
        name="local_sketch",
    )(g, e, p)


def total_kernel(parts_ref, out_ref):
    total = parts_ref[0]
    for i in range(1, parts_ref.shape[0]):
        total = total + parts_ref[i]
    for i in range(parts_ref.shape[0]):
        out_ref[i] = total


def total_for_all(parts):
    return pl.pallas_call(
        total_kernel,
        out_shape=jax.ShapeDtypeStruct(parts.shape, F32),
        compiler_params=params(),
        cost_estimate=pl.CostEstimate(flops=2 * 10**10, bytes_accessed=5 * 10**7, transcendentals=0),
        name="sketch_total",
    )(parts)


def factor_block(s12, s3, g_ref, e_ref, out_ref, side):
    width = out_ref.shape[0]
    for start in range(0, width, COLS):
        size = min(COLS, width - start)
        cols = pl.ds(pl.multiple_of(side * width + start, RANK), size)
        g, e = g_ref[:, cols], e_ref[:, cols]
        both = mm(s12, g) + mm(s12, e)
        out_ref[start : start + size, :] = (both[:RANK] + both[RANK:] + mm(s3, g + e)).T


def prepare_kernel(own_ref, other_ref, sketch_ref, s12_ref, s3_ref, gram_ref):
    core = lax.axis_index("core")
    half = own_ref.shape[0]
    sketch_ref[pl.ds(pl.multiple_of(core * half, half), half), :] = own_ref[...]
    sketch_ref[pl.ds(pl.multiple_of((1 - core) * half, half), half), :] = other_ref[...]
    hi, mid, low = split3(sketch_ref[...].T)
    s12_ref[:RANK, :] = hi
    s12_ref[RANK:, :] = mid
    s3_ref[...] = low
    square = mm(s12_ref[...], s12_ref[...], NT)
    cross = mm(hi, low, NT)
    gram_ref[...] = (
        square[:RANK, :RANK] + square[RANK:, RANK:]
        + (square[:RANK, RANK:] + square[RANK:, :RANK])
        + (cross + cross.T)
    )


def prepare(own, other):
    n = 2 * own.shape[0]
    return pl.pallas_call(
        prepare_kernel,
        out_shape=[
            jax.ShapeDtypeStruct((n, RANK), F32),
            jax.ShapeDtypeStruct((2 * RANK, n), BF16),
            jax.ShapeDtypeStruct((RANK, n), BF16),
            jax.ShapeDtypeStruct((RANK, RANK), F32),
        ],
        compiler_params=params(),
        name="prepare",
    )(own, other)


def factor_send_kernel(s12_ref, s3_ref, g_ref, e_ref, send_ref):
    factor_block(s12_ref[...], s3_ref[...], g_ref, e_ref, send_ref, 1 - lax.axis_index("core"))


def factor_keep_kernel(s12_ref, s3_ref, g_ref, e_ref, keep_ref):
    factor_block(s12_ref[...], s3_ref[...], g_ref, e_ref, keep_ref, lax.axis_index("core"))


def factor_half(kernel, name, s12, s3, g, e):
    return pl.pallas_call(
        kernel,
        out_shape=jax.ShapeDtypeStruct((g.shape[1] // 2, RANK), F32),
        compiler_params=params(),
        cost_estimate=pl.CostEstimate(flops=10**9, bytes_accessed=8 * 10**6, transcendentals=0),
        name=name,
    )(s12, s3, g, e)


def sum_in_order(parts, slots, out_ref):
    count = len(parts)
    place = lax.axis_index("fsdp")
    for k in range(count):
        slots[lax.rem(place + count - k, count)] = parts[k][...]
    total = slots[0]
    for k in range(1, count):
        total = total + slots[k]
    out_ref[...] = total


def across(tile, lane):
    return jnp.broadcast_to(tile[:, lane : lane + 1], tile.shape)


def down(tile, row):
    return jnp.broadcast_to(tile[row : row + 1, :], tile.shape)


def invert_cholesky(a_ref, b_ref, out_ref):
    tiles = RANK // 8
    lane = lax.broadcasted_iota(jnp.int32, (8, RANK), 1)
    row = lax.broadcasted_iota(jnp.int32, (8, RANK), 0)
    for t in range(tiles):
        b_ref[8 * t : 8 * t + 8, :] = jnp.where(lane == row + 8 * t, 1.0, 0.0)
    for t in range(tiles):
        here = slice(8 * t, 8 * t + 8)
        a_tile, b_tile = a_ref[here, :], b_ref[here, :]
        columns = [across(a_tile, 8 * t + k) for k in range(8)]
        value = {(i, k): down(columns[k], i) for k in range(8) for i in range(k, 8)}
        factor, inverse, root = {}, [], []
        for k in range(8):
            inverse.append(1.0 / value[k, k])
            root.append(lax.rsqrt(value[k, k]))
            for i in range(k + 1, 8):
                factor[i, k] = value[i, k] * inverse[k]
            for j in range(k + 1, 8):
                for i in range(j, 8):
                    value[i, j] = value[i, j] - factor[j, k] * value[i, k]
        a_rows = [down(a_tile, k) for k in range(8)]
        b_rows = [down(b_tile, k) for k in range(8)]
        for k in range(8):
            for i in range(k + 1, 8):
                a_rows[i] = a_rows[i] - factor[i, k] * a_rows[k]
                b_rows[i] = b_rows[i] - factor[i, k] * b_rows[k]
        for k in range(8):
            out_ref[8 * t + k : 8 * t + k + 1, :] = (b_rows[k] * root[k])[:1, :]
        for u in range(t + 1, tiles):
            there = slice(8 * u, 8 * u + 8)
            a_low, b_low = a_ref[there, :], b_ref[there, :]
            left = [across(a_low, 8 * t + k) for k in range(8)]
            for k in range(8):
                for i in range(k + 1, 8):
                    left[i] = left[i] - factor[i, k] * left[k]
                scaled = left[k] * inverse[k]
                a_low = a_low - scaled * a_rows[k]
                b_low = b_low - scaled * b_rows[k]
            a_ref[there, :] = a_low
            b_ref[there, :] = b_low


def pieces_kernel(parts_ref, out_ref):
    count = parts_ref.shape[0]
    total = parts_ref[0]
    for i in range(1, count):
        total = total + parts_ref[i]
    for i in range(count):
        out_ref[i] = total


def total_pieces(parts):
    return pl.pallas_call(
        pieces_kernel,
        out_shape=jax.ShapeDtypeStruct(parts.shape, F32),
        compiler_params=params(),
        name="total_pieces",
    )(parts)


def first_pass_kernel(*refs):
    grams, (sketch_ref, basis_ref, inv_ref, gram_ref, a_ref, b_ref, slots) = refs[:-7], refs[-7:]
    sum_in_order(grams, slots, a_ref)
    invert_cholesky(a_ref, b_ref, inv_ref)
    basis = mm32(sketch_ref[...], inv_ref[...], NT)
    basis_ref[...] = basis
    gram_ref[...] = mm32(basis, basis, TN)


def pass_scratch(count):
    return [pltpu.VMEM((RANK, RANK), F32)] * 2 + [pltpu.VMEM((count, RANK, RANK), F32)]


def pass_cost():
    return pl.CostEstimate(flops=4 * 10**9, bytes_accessed=2 * 10**7, transcendentals=0)


def first_pass(grams, sketch):
    square = jax.ShapeDtypeStruct((RANK, RANK), F32)
    return pl.pallas_call(
        first_pass_kernel,
        out_shape=[jax.ShapeDtypeStruct(sketch.shape, F32), square, square],
        scratch_shapes=pass_scratch(len(grams)),
        compiler_params=params(),
        cost_estimate=pass_cost(),
        name="first_pass",
    )(*grams, sketch)


def second_pass_kernel(*refs):
    grams, (basis_one_ref, inv_one_ref, basis_ref, inv_ref, two_ref, a_ref, b_ref, slots) = refs[:-8], refs[-8:]
    sum_in_order(grams, slots, a_ref)
    invert_cholesky(a_ref, b_ref, two_ref)
    basis_ref[...] = mm32(basis_one_ref[...], two_ref[...], NT)
    inv_ref[...] = mm32(two_ref[...], inv_one_ref[...])


def second_pass(grams, basis_one, inv_one):
    return pl.pallas_call(
        second_pass_kernel,
        out_shape=[
            jax.ShapeDtypeStruct(basis_one.shape, F32),
            jax.ShapeDtypeStruct(inv_one.shape, F32),
        ],
        scratch_shapes=[pltpu.VMEM((RANK, RANK), F32)] + pass_scratch(len(grams)),
        compiler_params=params(),
        cost_estimate=pass_cost(),
        name="second_pass",
    )(*grams, basis_one, inv_one)


def wide_nt(x, w):
    x1, x2, x3 = split3(x)
    w1, w2, w3 = split3(w)
    front = jnp.concatenate(
        [jnp.concatenate([w1, w1], axis=1), jnp.concatenate([w2, w2], axis=1)], axis=0
    )
    both = mm(jnp.concatenate([x1, x2], axis=1), front, NT)
    rest = mm(jnp.concatenate([x1, x3], axis=1), jnp.concatenate([w3, w1], axis=1), NT)
    return both[:, :RANK] + (both[:, RANK:] + rest)


def row_loads(g_hbm, e_hbm, g_ref, e_ref, sems, first, last):
    loads = []
    for k, start in enumerate(range(first, last, ROWS)):
        here, there = pl.ds(k * ROWS, ROWS), pl.ds(start, ROWS)
        loads.append(pltpu.make_async_copy(g_hbm.at[there], g_ref.at[here], sems.at[2 * k]))
        loads.append(pltpu.make_async_copy(e_hbm.at[there], e_ref.at[here], sems.at[2 * k + 1]))
    return loads


def fetch_kernel(basis_ref, g_hbm, e_hbm, q12_ref, g_ref, e_ref, sems):
    loads = row_loads(g_hbm, e_hbm, g_ref, e_ref, sems, 0, g_ref.shape[0])
    for load in loads:
        load.start()
    basis = basis_ref[...]
    hi = basis.astype(BF16)
    q12_ref[:, :RANK] = hi
    q12_ref[:, RANK:] = (basis - hi.astype(F32)).astype(BF16)
    for load in loads:
        load.wait()


def fetch(basis, g, e, top):
    n, m = g.shape
    rows = jax.ShapeDtypeStruct((top, m), BF16)
    return pl.pallas_call(
        fetch_kernel,
        in_specs=[VMEM_SPEC, HBM_SPEC, HBM_SPEC],
        out_specs=[VMEM_SPEC] * 3,
        out_shape=[jax.ShapeDtypeStruct((n, 2 * RANK), BF16), rows, rows],
        scratch_shapes=[pltpu.SemaphoreType.DMA((2 * (top // ROWS),))],
        compiler_params=params(FETCH_LIMIT),
        cost_estimate=pl.CostEstimate(flops=10**6, bytes_accessed=10**7, transcendentals=0),
        name="fetch",
    )(basis, g, e)


def residue_kernel(replicas, own_ref, other_ref, q12, inv_ref, g_top, e_top, g_hbm, e_hbm, right_hbm, new_hbm, halves, r11, r2, right_ref, new_ref, g_ref, e_ref, in_sems, out_sems):
    core = lax.axis_index("core")
    count, piece = own_ref.shape[0], own_ref.shape[1]
    n, m = new_ref.shape
    top = g_top.shape[0]
    loads = row_loads(g_hbm, e_hbm, g_ref, e_ref, in_sems, top, n)
    for load in loads:
        load.start()
    for i in range(count):
        halves[pl.ds(pl.multiple_of(core * (m // 2), 8) + i * piece, piece), :] = own_ref[i]
        halves[pl.ds(pl.multiple_of((1 - core) * (m // 2), 8) + i * piece, piece), :] = other_ref[i]
    right = wide_nt(halves[...], inv_ref[...]) * (1.0 / replicas)
    right_ref[...] = right
    right_copy = pltpu.make_async_copy(right_ref, right_hbm, out_sems.at[n // ROWS])
    right_copy.start()
    hi = right.astype(BF16)
    r11[:, :RANK] = hi
    r11[:, RANK:] = hi
    r2[...] = (right - hi.astype(F32)).astype(BF16)
    copies = []
    for k, first in enumerate(range(0, n, ROWS)):
        rows = pl.ds(first, ROWS)
        g_in, e_in, there = g_top, e_top, rows
        if first >= top:
            g_in, e_in, there = g_ref, e_ref, pl.ds(first - top, ROWS)
            loads[2 * ((first - top) // ROWS)].wait()
            loads[2 * ((first - top) // ROWS) + 1].wait()
        for start in range(0, m, COLS):
            cols = pl.ds(start, COLS)
            update = mm(q12[rows, :], r11[cols, :], NT) + mm(q12[rows, :RANK], r2[cols, :], NT)
            new_ref[rows, cols] = (g_in[there, cols].astype(F32) + e_in[there, cols].astype(F32) - update).astype(BF16)
        copies.append(pltpu.make_async_copy(new_ref.at[rows], new_hbm.at[rows], out_sems.at[k]))
        copies[-1].start()
    for copy in copies:
        copy.wait()
    right_copy.wait()


def residue(own, other, q12, inv, g_top, e_top, g, e, replicas):
    n, m = g.shape
    chunks, rest = n // ROWS, n - g_top.shape[0]
    return pl.pallas_call(
        functools.partial(residue_kernel, replicas),
        in_specs=[VMEM_SPEC] * 6 + [HBM_SPEC] * 2,
        out_specs=[HBM_SPEC] * 2,
        out_shape=[jax.ShapeDtypeStruct((m, RANK), F32), jax.ShapeDtypeStruct((n, m), BF16)],
        scratch_shapes=[
            pltpu.VMEM((m, RANK), F32),
            pltpu.VMEM((m, 2 * RANK), BF16),
            pltpu.VMEM((m, RANK), BF16),
            pltpu.VMEM((m, RANK), F32),
            pltpu.VMEM((n, m), BF16),
            pltpu.VMEM((rest, m), BF16),
            pltpu.VMEM((rest, m), BF16),
            pltpu.SemaphoreType.DMA((2 * (rest // ROWS),)),
            pltpu.SemaphoreType.DMA((chunks + 1,)),
        ],
        compiler_params=params(RESIDUE_LIMIT),
        name="residue",
    )(own, other, q12, inv, g_top, e_top, g, e)


def swap(x):
    return lax.ppermute(x, "core", [(0, 1), (1, 0)])


def round_fsdp(x, count):
    return [x] + [
        lax.ppermute(x, "fsdp", [(i, (i + k) % count) for i in range(count)]) for k in range(1, count)
    ]


def shards(gradients, errors, start_factor):
    g, e = gradients[0], errors[0]
    n = g.shape[0]
    ny, nx, nz = lax.axis_size("y"), lax.axis_size("fsdp"), lax.axis_size("tensor")
    keep, send = local_sketch(g, e, start_factor)
    pieces = (keep + swap(send)).reshape(ny * nz, -1, RANK)
    pieces = lax.all_to_all(pieces, ("y", "tensor"), 0, 0)
    own = lax.all_to_all(total_for_all(pieces), ("y", "tensor"), 0, 0).reshape(n // 2, RANK)
    sketch, s12, s3, gram = prepare(own, swap(own))
    grams = round_fsdp(gram, nx)
    send = factor_half(factor_send_kernel, "factor_send", s12, s3, g, e)
    got = swap(send)
    keep = factor_half(factor_keep_kernel, "factor_keep", s12, s3, g, e)
    parts = (keep + got).reshape(ny * nx, -1, RANK)
    parts = lax.all_to_all(parts, ("y", "fsdp"), 0, 0)
    basis_one, inv_one, gram = first_pass(grams, sketch)
    parts, gram = lax.optimization_barrier((parts, gram))
    grams = round_fsdp(gram, nx)
    own = lax.all_to_all(total_pieces(parts), ("y", "fsdp"), 0, 0)
    basis, inv = second_pass(grams, basis_one, inv_one)
    own, basis = lax.optimization_barrier((own, basis))
    other = swap(own)
    q12, g_top, e_top = fetch(basis, g, e, TOP)
    right_factor, new_errors = residue(own, other, q12, inv, g_top, e_top, g, e, 2 * ny)
    return (right_factor, new_errors[None])


def solution(mesh):
    shape = mesh.devices.shape
    split = Mesh(
        mesh.devices.reshape(shape[0] // 2, 2, *shape[1:]), ("y", "core", "fsdp", "tensor")
    )
    big = P(("y", "core"), "fsdp", "tensor")
    return jax.shard_map(
        shards,
        mesh=split,
        in_specs=(big, big, P("tensor", None)),
        out_specs=(P("tensor", None), big),
        check_vma=False,
    )
```

```python
import functools

import jax
import jax.numpy as jnp
from jax import lax
from jax.experimental import pallas as pl
from jax.experimental.pallas import tpu as pltpu
from jax.sharding import Mesh, PartitionSpec as P

F32, BF16 = jnp.float32, jnp.bfloat16
RANK = 128
ROWS = 256
COLS = 256
GROUP = 8
VMEM_LIMIT = 24 * 1024 * 1024
TOP = 384
FETCH_LIMIT = 51000000
RESIDUE_LIMIT = 51000000
STREAM_LIMIT = 55500000
NT = (((1,), (1,)), ((), ()))
NN = (((1,), (0,)), ((), ()))


def mm(a, b, dims=NN):
    return lax.dot_general(a, b, dims, preferred_element_type=F32)


def mm32(a, b, dims=NN):
    return lax.dot_general(a, b, dims, precision=lax.Precision.HIGHEST, preferred_element_type=F32)


def split3(x):
    hi = x.astype(BF16)
    rest = x - hi.astype(F32)
    mid = rest.astype(BF16)
    low = (rest - mid.astype(F32)).astype(BF16)
    return hi, mid, low


VMEM_SPEC = pl.BlockSpec(memory_space=pltpu.VMEM)
HBM_SPEC = pl.BlockSpec(memory_space=pltpu.HBM)


def params(limit=VMEM_LIMIT):
    return pltpu.CompilerParams(vmem_limit_bytes=limit)


def chunks_of(first, last, tail):
    blocks = []
    while first < last:
        size = min(ROWS, last - first)
        if tail and first + size == last and size == ROWS:
            size = ROWS // 2
        blocks.append((first, size))
        first += size
    return blocks


def sketch_kernel(g_hbm, e_hbm, p_hbm, keep_ref, send_ref, both_ref, p_ref, p12, p3, sems):
    n = g_hbm.shape[0]
    steps, ahead = n // ROWS, 2
    core = lax.axis_index("core")

    def load(i):
        rows = pl.ds(i * ROWS, ROWS)
        return (
            pltpu.make_async_copy(g_hbm.at[rows], both_ref.at[pl.ds(2 * i * ROWS, ROWS)], sems.at[2 * i]),
            pltpu.make_async_copy(e_hbm.at[rows], both_ref.at[pl.ds((2 * i + 1) * ROWS, ROWS)], sems.at[2 * i + 1]),
        )

    half = p_ref.shape[0] // 2
    halves = [pl.ds(0, half), pl.ds(half, half)]
    firsts = [
        pltpu.make_async_copy(p_hbm.at[rows], p_ref.at[rows], sems.at[2 * steps + k])
        for k, rows in enumerate(halves)
    ]
    for copy in firsts:
        copy.start()
    copies = [load(i) for i in range(steps)]
    for i in range(ahead):
        copies[i][0].start()
        copies[i][1].start()
    for copy, rows in zip(firsts, halves):
        copy.wait()
        hi, mid, low = split3(p_ref[rows, :])
        p12[rows, :RANK] = hi
        p12[rows, RANK:] = mid
        p3[rows, :] = low
    for i in range(steps):
        copies[i][0].wait()
        copies[i][1].wait()
        if i + ahead < steps:
            copies[i + ahead][0].start()
            copies[i + ahead][1].start()
        stacked = both_ref[pl.ds(2 * i * ROWS, 2 * ROWS), :]
        wide = mm(stacked, p12[...])
        wide = wide[:ROWS] + wide[ROWS:]
        block = wide[:, :RANK] + wide[:, RANK:] + mm(stacked[:ROWS] + stacked[ROWS:], p3[...])
        half = i // (steps // 2)
        place = pl.ds((i - half * (steps // 2)) * ROWS, ROWS)

        @pl.when(core == half)
        def _():
            keep_ref[place, :] = block

        @pl.when(core != half)
        def _():
            send_ref[place, :] = block


def local_sketch(g, e, p):
    n, m = g.shape
    half = jax.ShapeDtypeStruct((n // 2, RANK), F32)
    return pl.pallas_call(
        sketch_kernel,
        in_specs=[HBM_SPEC] * 3,
        out_specs=[VMEM_SPEC] * 2,
        out_shape=[half, half],
        scratch_shapes=[
            pltpu.VMEM((2 * n, m), BF16),
            pltpu.VMEM((m, RANK), F32),
            pltpu.VMEM((m, 2 * RANK), BF16),
            pltpu.VMEM((m, RANK), BF16),
            pltpu.SemaphoreType.DMA((2 * (n // ROWS) + 2,)),
        ],
        compiler_params=params(STREAM_LIMIT),
        name="local_sketch",
    )(g, e, p)


def total_kernel(parts_ref, out_ref):
    total = parts_ref[0]
    for i in range(1, parts_ref.shape[0]):
        total = total + parts_ref[i]
    for i in range(parts_ref.shape[0]):
        out_ref[i] = total


def total_for_all(parts):
    return pl.pallas_call(
        total_kernel,
        out_shape=jax.ShapeDtypeStruct(parts.shape, F32),
        compiler_params=params(),
        cost_estimate=pl.CostEstimate(flops=2 * 10**10, bytes_accessed=5 * 10**7, transcendentals=0),
        name="sketch_total",
    )(parts)


def tiles_of(width):
    return [(start, min(COLS, width - start)) for start in range(0, width, COLS)]


def factor_tile(s12_ref, s3_ref, g_ref, e_ref, side, width, start, size):
    cols = pl.ds(pl.multiple_of(side * width + start, RANK), size)
    g, e = g_ref[:, cols], e_ref[:, cols]
    both = mm(s12_ref[...], g) + mm(s12_ref[...], e)
    return (both[:RANK] + both[RANK:] + mm(s3_ref[...], g + e)).T


def wide_nt(x, w):
    x1, x2, x3 = split3(x)
    w1, w2, w3 = split3(w)
    front = jnp.concatenate(
        [jnp.concatenate([w1, w1], axis=1), jnp.concatenate([w2, w2], axis=1)], axis=0
    )
    both = mm(jnp.concatenate([x1, x2], axis=1), front, NT)
    rest = mm(jnp.concatenate([x1, x3], axis=1), jnp.concatenate([w3, w1], axis=1), NT)
    return both[:, :RANK] + (both[:, RANK:] + rest)


def square_nt(hi_mid, low):
    square = mm(hi_mid, hi_mid, NT)
    cross = mm(hi_mid[:RANK], low, NT)
    return (
        square[:RANK, :RANK] + square[RANK:, RANK:]
        + (square[:RANK, RANK:] + square[RANK:, :RANK])
        + (cross + cross.T)
    )


def prepare_kernel(own_ref, other_ref, sketch_ref, s12_ref, s3_ref, gram_ref):
    core = lax.axis_index("core")
    half = own_ref.shape[0]
    sketch_ref[pl.ds(pl.multiple_of(core * half, half), half), :] = own_ref[...]
    sketch_ref[pl.ds(pl.multiple_of((1 - core) * half, half), half), :] = other_ref[...]
    hi, mid, low = split3(sketch_ref[...].T)
    s12_ref[:RANK, :] = hi
    s12_ref[RANK:, :] = mid
    s3_ref[...] = low
    gram_ref[...] = square_nt(s12_ref[...], low)


def prepare(own, other):
    n = 2 * own.shape[0]
    return pl.pallas_call(
        prepare_kernel,
        out_shape=[
            jax.ShapeDtypeStruct((n, RANK), F32),
            jax.ShapeDtypeStruct((2 * RANK, n), BF16),
            jax.ShapeDtypeStruct((RANK, n), BF16),
            jax.ShapeDtypeStruct((RANK, RANK), F32),
        ],
        compiler_params=params(),
        name="prepare",
    )(own, other)


def factor_send_kernel(s12_ref, s3_ref, g_ref, e_ref, send_ref):
    side, width = 1 - lax.axis_index("core"), send_ref.shape[0]
    for start, size in tiles_of(width):
        send_ref[start : start + size, :] = factor_tile(s12_ref, s3_ref, g_ref, e_ref, side, width, start, size)


def factor_keep_kernel(s12_ref, s3_ref, g_ref, e_ref, got_ref, out_hbm, sum_ref, sems):
    side, width = lax.axis_index("core"), got_ref.shape[0]
    copies = []
    for k, (start, size) in enumerate(tiles_of(width)):
        rows = pl.ds(start, size)
        sum_ref[rows, :] = got_ref[rows, :] + factor_tile(s12_ref, s3_ref, g_ref, e_ref, side, width, start, size)
        copies.append(pltpu.make_async_copy(sum_ref.at[rows], out_hbm.at[rows], sems.at[k]))
        copies[-1].start()
    for copy in copies:
        copy.wait()


def factor_cost():
    return pl.CostEstimate(flops=10**9, bytes_accessed=8 * 10**6, transcendentals=0)


def factor_send(s12, s3, g, e):
    return pl.pallas_call(
        factor_send_kernel,
        out_shape=jax.ShapeDtypeStruct((g.shape[1] // 2, RANK), F32),
        compiler_params=params(),
        cost_estimate=factor_cost(),
        name="factor_send",
    )(s12, s3, g, e)


def factor_keep(s12, s3, g, e, got):
    return pl.pallas_call(
        factor_keep_kernel,
        in_specs=[VMEM_SPEC] * 5,
        out_specs=HBM_SPEC,
        out_shape=jax.ShapeDtypeStruct(got.shape, F32),
        scratch_shapes=[
            pltpu.VMEM(got.shape, F32),
            pltpu.SemaphoreType.DMA((len(tiles_of(got.shape[0])),)),
        ],
        compiler_params=params(),
        cost_estimate=factor_cost(),
        name="factor_keep",
    )(s12, s3, g, e, got)


def sum_in_order(parts, slots, out_ref):
    count = len(parts)
    place = lax.axis_index("fsdp")
    for k in range(count):
        slots[lax.rem(place + count - k, count)] = parts[k][...]
    total = slots[0]
    for k in range(1, count):
        total = total + slots[k]
    out_ref[...] = total


def across(tile, lane):
    return jnp.broadcast_to(tile[:, lane : lane + 1], tile.shape)


def down(tile, row):
    return jnp.broadcast_to(tile[row : row + 1, :], tile.shape)


def tree_sum(terms):
    while len(terms) > 1:
        terms = [terms[i] + terms[i + 1] for i in range(0, len(terms), 2)]
    return terms[0]


def invert_cholesky(a_ref, b_ref, out_ref):
    tiles = RANK // 8
    lane = lax.broadcasted_iota(jnp.int32, (8, RANK), 1)
    row = lax.broadcasted_iota(jnp.int32, (8, RANK), 0)
    for t in range(tiles):
        b_ref[8 * t : 8 * t + 8, :] = jnp.where(lane == row + 8 * t, 1.0, 0.0)
    for first in range(0, RANK, GROUP):
        t, skip = first // 8, first % 8
        here = slice(8 * t, 8 * t + 8)
        a_tile, b_tile = a_ref[here, :], b_ref[here, :]
        columns = [across(a_tile, first + k) for k in range(GROUP)]
        value = {(i, k): down(columns[k], skip + i) for k in range(GROUP) for i in range(k, GROUP)}
        factor, inverse, root = {}, [], []
        for k in range(GROUP):
            inverse.append(1.0 / value[k, k])
            root.append(lax.rsqrt(value[k, k]))
            for i in range(k + 1, GROUP):
                factor[i, k] = value[i, k] * inverse[k]
            for j in range(k + 1, GROUP):
                for i in range(j, GROUP):
                    value[i, j] = value[i, j] - factor[j, k] * value[i, k]
        a_rows = [down(a_tile, skip + k) for k in range(GROUP)]
        b_rows = [down(b_tile, skip + k) for k in range(GROUP)]
        for k in range(GROUP):
            for i in range(k + 1, GROUP):
                a_rows[i] = a_rows[i] - factor[i, k] * a_rows[k]
                b_rows[i] = b_rows[i] - factor[i, k] * b_rows[k]
        for k in range(GROUP):
            out_ref[first + k : first + k + 1, :] = (b_rows[k] * root[k])[:1, :]
        a_rows = [a_rows[k] * inverse[k] for k in range(GROUP)]
        b_rows = [b_rows[k] * inverse[k] for k in range(GROUP)]
        for u in range(t if skip + GROUP < 8 else t + 1, tiles):
            there = slice(8 * u, 8 * u + 8)
            a_low, b_low = a_ref[there, :], b_ref[there, :]
            left = [across(a_low, first + k) for k in range(GROUP)]
            for k in range(GROUP):
                for i in range(k + 1, GROUP):
                    left[i] = left[i] - factor[i, k] * left[k]
            a_ref[there, :] = a_low - tree_sum([left[k] * a_rows[k] for k in range(GROUP)])
            b_ref[there, :] = b_low - tree_sum([left[k] * b_rows[k] for k in range(GROUP)])


def pieces_kernel(parts_ref, out_ref):
    count = parts_ref.shape[0]
    total = parts_ref[0]
    for i in range(1, count):
        total = total + parts_ref[i]
    for i in range(count):
        out_ref[i] = total


def total_pieces(parts):
    return pl.pallas_call(
        pieces_kernel,
        out_shape=jax.ShapeDtypeStruct(parts.shape, F32),
        compiler_params=params(),
        name="total_pieces",
    )(parts)


def first_pass_kernel(*refs):
    grams, (sketch_ref, basis_ref, inv_ref, gram_ref, a_ref, b_ref, slots) = refs[:-7], refs[-7:]
    sum_in_order(grams, slots, a_ref)
    invert_cholesky(a_ref, b_ref, inv_ref)
    basis = wide_nt(sketch_ref[...], inv_ref[...])
    basis_ref[...] = basis
    hi, mid, low = split3(basis.T)
    gram_ref[...] = square_nt(jnp.concatenate([hi, mid], axis=0), low)


def pass_scratch(count):
    return [pltpu.VMEM((RANK, RANK), F32)] * 2 + [pltpu.VMEM((count, RANK, RANK), F32)]


def pass_cost():
    return pl.CostEstimate(flops=4 * 10**9, bytes_accessed=2 * 10**7, transcendentals=0)


def first_pass(grams, sketch):
    square = jax.ShapeDtypeStruct((RANK, RANK), F32)
    return pl.pallas_call(
        first_pass_kernel,
        out_shape=[jax.ShapeDtypeStruct(sketch.shape, F32), square, square],
        scratch_shapes=pass_scratch(len(grams)),
        compiler_params=params(),
        cost_estimate=pass_cost(),
        name="first_pass",
    )(*grams, sketch)


def second_pass_kernel(*refs):
    grams, (basis_one_ref, inv_one_ref, basis_ref, inv_ref, two_ref, a_ref, b_ref, slots) = refs[:-8], refs[-8:]
    sum_in_order(grams, slots, a_ref)
    invert_cholesky(a_ref, b_ref, two_ref)
    basis_ref[...] = wide_nt(basis_one_ref[...], two_ref[...])
    inv_ref[...] = mm32(two_ref[...], inv_one_ref[...])


def second_pass(grams, basis_one, inv_one):
    return pl.pallas_call(
        second_pass_kernel,
        out_shape=[
            jax.ShapeDtypeStruct(basis_one.shape, F32),
            jax.ShapeDtypeStruct(inv_one.shape, F32),
        ],
        scratch_shapes=[pltpu.VMEM((RANK, RANK), F32)] + pass_scratch(len(grams)),
        compiler_params=params(),
        cost_estimate=pass_cost(),
        name="second_pass",
    )(*grams, basis_one, inv_one)


def row_loads(g_hbm, e_hbm, g_ref, e_ref, sems, blocks):
    loads = []
    for k, (start, size) in enumerate(blocks):
        here, there = pl.ds(start - blocks[0][0], size), pl.ds(start, size)
        loads.append(pltpu.make_async_copy(g_hbm.at[there], g_ref.at[here], sems.at[2 * k]))
        loads.append(pltpu.make_async_copy(e_hbm.at[there], e_ref.at[here], sems.at[2 * k + 1]))
    return loads


def fetch_kernel(basis_ref, g_hbm, e_hbm, q3_ref, g_ref, e_ref, sems):
    loads = row_loads(g_hbm, e_hbm, g_ref, e_ref, sems, chunks_of(0, g_ref.shape[0], False))
    for load in loads:
        load.start()
    basis = basis_ref[...]
    hi = basis.astype(BF16)
    q3_ref[:, :RANK] = hi
    q3_ref[:, RANK : 2 * RANK] = (basis - hi.astype(F32)).astype(BF16)
    q3_ref[:, 2 * RANK :] = hi
    for load in loads:
        load.wait()


def fetch(basis, g, e, top):
    n, m = g.shape
    rows = jax.ShapeDtypeStruct((top, m), BF16)
    return pl.pallas_call(
        fetch_kernel,
        in_specs=[VMEM_SPEC, HBM_SPEC, HBM_SPEC],
        out_specs=[VMEM_SPEC] * 3,
        out_shape=[jax.ShapeDtypeStruct((n, 3 * RANK), BF16), rows, rows],
        scratch_shapes=[pltpu.SemaphoreType.DMA((2 * len(chunks_of(0, top, False)),))],
        compiler_params=params(FETCH_LIMIT),
        cost_estimate=pl.CostEstimate(flops=10**6, bytes_accessed=10**7, transcendentals=0),
        name="fetch",
    )(basis, g, e)


def residue_kernel(replicas, own_ref, other_ref, q3, inv_ref, g_top, e_top, g_hbm, e_hbm, right_hbm, new_hbm, halves, right3, right_ref, new_ref, g_ref, e_ref, in_sems, out_sems):
    core = lax.axis_index("core")
    count, piece = own_ref.shape[0], own_ref.shape[1]
    n, m = new_ref.shape
    top = g_top.shape[0]
    early, late = chunks_of(0, top, False), chunks_of(top, n, True)
    loads = row_loads(g_hbm, e_hbm, g_ref, e_ref, in_sems, late)
    for load in loads:
        load.start()
    for i in range(count):
        halves[pl.ds(pl.multiple_of(core * (m // 2), 8) + i * piece, piece), :] = own_ref[i]
        halves[pl.ds(pl.multiple_of((1 - core) * (m // 2), 8) + i * piece, piece), :] = other_ref[i]
    right = wide_nt(halves[...], inv_ref[...]) * (1.0 / replicas)
    right_ref[...] = right
    right_copy = pltpu.make_async_copy(right_ref, right_hbm, out_sems.at[len(early) + len(late)])
    right_copy.start()
    hi = right.astype(BF16)
    right3[:, :RANK] = hi
    right3[:, RANK : 2 * RANK] = hi
    right3[:, 2 * RANK :] = (right - hi.astype(F32)).astype(BF16)
    copies = []
    for k, (first, size) in enumerate(early + late):
        rows = pl.ds(first, size)
        g_in, e_in, there = g_top, e_top, rows
        if first >= top:
            g_in, e_in, there = g_ref, e_ref, pl.ds(first - top, size)
            loads[2 * (k - len(early))].wait()
            loads[2 * (k - len(early)) + 1].wait()
        for start in range(0, m, COLS):
            cols = pl.ds(start, COLS)
            update = mm(q3[rows, :], right3[cols, :], NT)
            new_ref[rows, cols] = (g_in[there, cols].astype(F32) + e_in[there, cols].astype(F32) - update).astype(BF16)
        copies.append(pltpu.make_async_copy(new_ref.at[rows], new_hbm.at[rows], out_sems.at[k]))
        copies[-1].start()
    for copy in copies:
        copy.wait()
    right_copy.wait()


def residue(own, other, q3, inv, g_top, e_top, g, e, replicas):
    n, m = g.shape
    top = g_top.shape[0]
    early, late = chunks_of(0, top, False), chunks_of(top, n, True)
    return pl.pallas_call(
        functools.partial(residue_kernel, replicas),
        in_specs=[VMEM_SPEC] * 6 + [HBM_SPEC] * 2,
        out_specs=[HBM_SPEC] * 2,
        out_shape=[jax.ShapeDtypeStruct((m, RANK), F32), jax.ShapeDtypeStruct((n, m), BF16)],
        scratch_shapes=[
            pltpu.VMEM((m, RANK), F32),
            pltpu.VMEM((m, 3 * RANK), BF16),
            pltpu.VMEM((m, RANK), F32),
            pltpu.VMEM((n, m), BF16),
            pltpu.VMEM((n - top, m), BF16),
            pltpu.VMEM((n - top, m), BF16),
            pltpu.SemaphoreType.DMA((2 * len(late),)),
            pltpu.SemaphoreType.DMA((len(early) + len(late) + 1,)),
        ],
        compiler_params=params(RESIDUE_LIMIT),
        name="residue",
    )(own, other, q3, inv, g_top, e_top, g, e)


def swap(x):
    return lax.ppermute(x, "core", [(0, 1), (1, 0)])


def round_fsdp(x, count):
    return [x] + [
        lax.ppermute(x, "fsdp", [(i, (i + k) % count) for i in range(count)]) for k in range(1, count)
    ]


def shards(gradients, errors, start_factor):
    g, e = gradients[0], errors[0]
    n = g.shape[0]
    ny, nx, nz = lax.axis_size("y"), lax.axis_size("fsdp"), lax.axis_size("tensor")
    keep, send = local_sketch(g, e, start_factor)
    pieces = (keep + swap(send)).reshape(ny * nz, -1, RANK)
    pieces = lax.all_to_all(pieces, ("y", "tensor"), 0, 0)
    own = lax.all_to_all(total_for_all(pieces), ("y", "tensor"), 0, 0).reshape(n // 2, RANK)
    sketch, s12, s3, gram = prepare(own, swap(own))
    grams = round_fsdp(gram, nx)
    got = swap(factor_send(s12, s3, g, e))
    parts = factor_keep(s12, s3, g, e, got).reshape(ny * nx, -1, RANK)
    parts = lax.all_to_all(parts, ("y", "fsdp"), 0, 0)
    basis_one, inv_one, gram = first_pass(grams, sketch)
    parts, _ = lax.optimization_barrier((parts, gram))
    grams = round_fsdp(gram, nx)
    own = lax.all_to_all(total_pieces(parts), ("y", "fsdp"), 0, 0)
    basis, inv = second_pass(grams, basis_one, inv_one)
    own, basis = lax.optimization_barrier((own, basis))
    other = swap(own)
    q3, g_top, e_top = fetch(basis, g, e, TOP)
    right_factor, new_errors = residue(own, other, q3, inv, g_top, e_top, g, e, 2 * ny)
    return (right_factor, new_errors[None])


def solution(mesh):
    shape = mesh.devices.shape
    split = Mesh(
        mesh.devices.reshape(shape[0] // 2, 2, *shape[1:]), ("y", "core", "fsdp", "tensor")
    )
    big = P(("y", "core"), "fsdp", "tensor")
    return jax.shard_map(
        shards,
        mesh=split,
        in_specs=(big, big, P("tensor", None)),
        out_specs=(P("tensor", None), big),
        check_vma=False,
    )
```

```python
import functools

import jax
import jax.numpy as jnp
from jax import lax
from jax.experimental import pallas as pl
from jax.experimental.pallas import tpu as pltpu
from jax.sharding import Mesh, PartitionSpec as P

F32, BF16 = jnp.float32, jnp.bfloat16
RANK = 128
ROWS = 256
COLS = 256
GROUP = 8
VMEM_LIMIT = 24 * 1024 * 1024
TOP = 384
FETCH_LIMIT = 51000000
RESIDUE_LIMIT = 51000000
STREAM_LIMIT = 55500000
NT = (((1,), (1,)), ((), ()))
NN = (((1,), (0,)), ((), ()))


def mm(a, b, dims=NN):
    return lax.dot_general(a, b, dims, preferred_element_type=F32)


def mm32(a, b, dims=NN):
    return lax.dot_general(a, b, dims, precision=lax.Precision.HIGHEST, preferred_element_type=F32)


def split3(x):
    hi = x.astype(BF16)
    rest = x - hi.astype(F32)
    mid = rest.astype(BF16)
    low = (rest - mid.astype(F32)).astype(BF16)
    return hi, mid, low


VMEM_SPEC = pl.BlockSpec(memory_space=pltpu.VMEM)
HBM_SPEC = pl.BlockSpec(memory_space=pltpu.HBM)


def params(limit=VMEM_LIMIT):
    return pltpu.CompilerParams(vmem_limit_bytes=limit)


def chunks_of(first, last, tail):
    blocks = []
    while first < last:
        size = min(ROWS, last - first)
        if tail and first + size == last and size == ROWS:
            size = ROWS // 2
        blocks.append((first, size))
        first += size
    return blocks


def sketch_kernel(g_hbm, e_hbm, p_hbm, keep_ref, send_ref, both_ref, p_ref, p12, p3, sems):
    n = g_hbm.shape[0]
    steps, ahead = n // ROWS, 2
    core = lax.axis_index("core")

    def load(i):
        rows = pl.ds(i * ROWS, ROWS)
        return (
            pltpu.make_async_copy(g_hbm.at[rows], both_ref.at[pl.ds(2 * i * ROWS, ROWS)], sems.at[2 * i]),
            pltpu.make_async_copy(e_hbm.at[rows], both_ref.at[pl.ds((2 * i + 1) * ROWS, ROWS)], sems.at[2 * i + 1]),
        )

    half = p_ref.shape[0] // 2
    halves = [pl.ds(0, half), pl.ds(half, half)]
    firsts = [
        pltpu.make_async_copy(p_hbm.at[rows], p_ref.at[rows], sems.at[2 * steps + k])
        for k, rows in enumerate(halves)
    ]
    for copy in firsts:
        copy.start()
    copies = [load(i) for i in range(steps)]
    for i in range(ahead):
        copies[i][0].start()
        copies[i][1].start()
    for copy, rows in zip(firsts, halves):
        copy.wait()
        hi, mid, low = split3(p_ref[rows, :])
        p12[rows, :RANK] = hi
        p12[rows, RANK:] = mid
        p3[rows, :] = low
    for i in range(steps):
        copies[i][0].wait()
        copies[i][1].wait()
        if i + ahead < steps:
            copies[i + ahead][0].start()
            copies[i + ahead][1].start()
        stacked = both_ref[pl.ds(2 * i * ROWS, 2 * ROWS), :]
        wide = mm(stacked, p12[...])
        wide = wide[:ROWS] + wide[ROWS:]
        block = wide[:, :RANK] + wide[:, RANK:] + mm(stacked[:ROWS] + stacked[ROWS:], p3[...])
        half = i // (steps // 2)
        place = pl.ds((i - half * (steps // 2)) * ROWS, ROWS)

        @pl.when(core == half)
        def _():
            keep_ref[place, :] = block

        @pl.when(core != half)
        def _():
            send_ref[place, :] = block


def local_sketch(g, e, p):
    n, m = g.shape
    half = jax.ShapeDtypeStruct((n // 2, RANK), F32)
    return pl.pallas_call(
        sketch_kernel,
        in_specs=[HBM_SPEC] * 3,
        out_specs=[VMEM_SPEC] * 2,
        out_shape=[half, half],
        scratch_shapes=[
            pltpu.VMEM((2 * n, m), BF16),
            pltpu.VMEM((m, RANK), F32),
            pltpu.VMEM((m, 2 * RANK), BF16),
            pltpu.VMEM((m, RANK), BF16),
            pltpu.SemaphoreType.DMA((2 * (n // ROWS) + 2,)),
        ],
        compiler_params=params(STREAM_LIMIT),
        name="local_sketch",
    )(g, e, p)


def total_kernel(parts_ref, out_ref):
    total = parts_ref[0]
    for i in range(1, parts_ref.shape[0]):
        total = total + parts_ref[i]
    for i in range(parts_ref.shape[0]):
        out_ref[i] = total


def total_for_all(parts):
    return pl.pallas_call(
        total_kernel,
        out_shape=jax.ShapeDtypeStruct(parts.shape, F32),
        compiler_params=params(),
        cost_estimate=pl.CostEstimate(flops=2 * 10**10, bytes_accessed=5 * 10**7, transcendentals=0),
        name="sketch_total",
    )(parts)


def tiles_of(width):
    return [(start, min(COLS, width - start)) for start in range(0, width, COLS)]


def factor_tile(s12_ref, s3_ref, g_ref, e_ref, side, width, start, size):
    cols = pl.ds(pl.multiple_of(side * width + start, RANK), size)
    g, e = g_ref[:, cols], e_ref[:, cols]
    both = mm(s12_ref[...], g) + mm(s12_ref[...], e)
    return (both[:RANK] + both[RANK:] + mm(s3_ref[...], g + e)).T


def wide_nt(x, w):
    x1, x2, x3 = split3(x)
    w1, w2, w3 = split3(w)
    front = jnp.concatenate(
        [jnp.concatenate([w1, w1], axis=1), jnp.concatenate([w2, w2], axis=1)], axis=0
    )
    both = mm(jnp.concatenate([x1, x2], axis=1), front, NT)
    rest = mm(jnp.concatenate([x1, x3], axis=1), jnp.concatenate([w3, w1], axis=1), NT)
    return both[:, :RANK] + (both[:, RANK:] + rest)


def wide_turned(w, x12, x1, x3):
    w1, w2, w3 = split3(w)
    front = jnp.concatenate(
        [jnp.concatenate([w1, w1], axis=1), jnp.concatenate([w2, w2], axis=1)], axis=0
    )
    both = mm(front, x12)
    rest = mm(w1, x3) + mm(w3, x1)
    return both[:RANK] + (both[RANK:] + rest)


def square_nt(hi_mid, low):
    square = mm(hi_mid, hi_mid, NT)
    cross = mm(hi_mid[:RANK], low, NT)
    return (
        square[:RANK, :RANK] + square[RANK:, RANK:]
        + (square[:RANK, RANK:] + square[RANK:, :RANK])
        + (cross + cross.T)
    )


def prepare_kernel(own_ref, other_ref, s12_ref, s3_ref, gram_ref, sketch_ref):
    core = lax.axis_index("core")
    half = own_ref.shape[0]
    sketch_ref[pl.ds(pl.multiple_of(core * half, half), half), :] = own_ref[...]
    sketch_ref[pl.ds(pl.multiple_of((1 - core) * half, half), half), :] = other_ref[...]
    hi, mid, low = split3(sketch_ref[...].T)
    s12_ref[:RANK, :] = hi
    s12_ref[RANK:, :] = mid
    s3_ref[...] = low
    gram_ref[...] = square_nt(s12_ref[...], low)


def prepare(own, other):
    n = 2 * own.shape[0]
    return pl.pallas_call(
        prepare_kernel,
        out_shape=[
            jax.ShapeDtypeStruct((2 * RANK, n), BF16),
            jax.ShapeDtypeStruct((RANK, n), BF16),
            jax.ShapeDtypeStruct((RANK, RANK), F32),
        ],
        scratch_shapes=[pltpu.VMEM((n, RANK), F32)],
        compiler_params=params(),
        name="prepare",
    )(own, other)


def factor_send_kernel(s12_ref, s3_ref, g_ref, e_ref, send_ref):
    side, width = 1 - lax.axis_index("core"), send_ref.shape[0]
    for start, size in tiles_of(width):
        send_ref[start : start + size, :] = factor_tile(s12_ref, s3_ref, g_ref, e_ref, side, width, start, size)


def factor_keep_kernel(s12_ref, s3_ref, g_ref, e_ref, got_ref, out_hbm, sum_ref, sems):
    side, width = lax.axis_index("core"), got_ref.shape[0]
    copies = []
    for k, (start, size) in enumerate(tiles_of(width)):
        rows = pl.ds(start, size)
        sum_ref[rows, :] = got_ref[rows, :] + factor_tile(s12_ref, s3_ref, g_ref, e_ref, side, width, start, size)
        copies.append(pltpu.make_async_copy(sum_ref.at[rows], out_hbm.at[rows], sems.at[k]))
        copies[-1].start()
    for copy in copies:
        copy.wait()


def factor_cost():
    return pl.CostEstimate(flops=10**9, bytes_accessed=8 * 10**6, transcendentals=0)


def factor_send(s12, s3, g, e):
    return pl.pallas_call(
        factor_send_kernel,
        out_shape=jax.ShapeDtypeStruct((g.shape[1] // 2, RANK), F32),
        compiler_params=params(),
        cost_estimate=factor_cost(),
        name="factor_send",
    )(s12, s3, g, e)


def factor_keep(s12, s3, g, e, got):
    return pl.pallas_call(
        factor_keep_kernel,
        in_specs=[VMEM_SPEC] * 5,
        out_specs=HBM_SPEC,
        out_shape=jax.ShapeDtypeStruct(got.shape, F32),
        scratch_shapes=[
            pltpu.VMEM(got.shape, F32),
            pltpu.SemaphoreType.DMA((len(tiles_of(got.shape[0])),)),
        ],
        compiler_params=params(),
        cost_estimate=factor_cost(),
        name="factor_keep",
    )(s12, s3, g, e, got)


def sum_in_order(parts, slots, out_ref):
    count = len(parts)
    place = lax.axis_index("fsdp")
    for k in range(count):
        slots[lax.rem(place + count - k, count)] = parts[k][...]
    total = slots[0]
    for k in range(1, count):
        total = total + slots[k]
    out_ref[...] = total


def across(tile, lane):
    return jnp.broadcast_to(tile[:, lane : lane + 1], tile.shape)


def down(tile, row):
    return jnp.broadcast_to(tile[row : row + 1, :], tile.shape)


def tree_sum(terms):
    while len(terms) > 1:
        terms = [terms[i] + terms[i + 1] for i in range(0, len(terms), 2)]
    return terms[0]


def invert_cholesky(a_ref, b_ref, out_ref):
    tiles = RANK // 8
    lane = lax.broadcasted_iota(jnp.int32, (8, RANK), 1)
    row = lax.broadcasted_iota(jnp.int32, (8, RANK), 0)
    for t in range(tiles):
        b_ref[8 * t : 8 * t + 8, :] = jnp.where(lane == row + 8 * t, 1.0, 0.0)
    for first in range(0, RANK, GROUP):
        t, skip = first // 8, first % 8
        here = slice(8 * t, 8 * t + 8)
        a_tile, b_tile = a_ref[here, :], b_ref[here, :]
        columns = [across(a_tile, first + k) for k in range(GROUP)]
        value = {(i, k): down(columns[k], skip + i) for k in range(GROUP) for i in range(k, GROUP)}
        factor, inverse, root = {}, [], []
        for k in range(GROUP):
            inverse.append(1.0 / value[k, k])
            root.append(lax.rsqrt(value[k, k]))
            for i in range(k + 1, GROUP):
                factor[i, k] = value[i, k] * inverse[k]
            for j in range(k + 1, GROUP):
                for i in range(j, GROUP):
                    value[i, j] = value[i, j] - factor[j, k] * value[i, k]
        a_rows = [down(a_tile, skip + k) for k in range(GROUP)]
        b_rows = [down(b_tile, skip + k) for k in range(GROUP)]
        for k in range(GROUP):
            for i in range(k + 1, GROUP):
                a_rows[i] = a_rows[i] - factor[i, k] * a_rows[k]
                b_rows[i] = b_rows[i] - factor[i, k] * b_rows[k]
        for k in range(GROUP):
            out_ref[first + k : first + k + 1, :] = (b_rows[k] * root[k])[:1, :]
        a_rows = [a_rows[k] * inverse[k] for k in range(GROUP)]
        b_rows = [b_rows[k] * inverse[k] for k in range(GROUP)]
        for u in range(t if skip + GROUP < 8 else t + 1, tiles):
            there = slice(8 * u, 8 * u + 8)
            a_low, b_low = a_ref[there, :], b_ref[there, :]
            left = [across(a_low, first + k) for k in range(GROUP)]
            for k in range(GROUP):
                for i in range(k + 1, GROUP):
                    left[i] = left[i] - factor[i, k] * left[k]
            a_ref[there, :] = a_low - tree_sum([left[k] * a_rows[k] for k in range(GROUP)])
            b_ref[there, :] = b_low - tree_sum([left[k] * b_rows[k] for k in range(GROUP)])


def pieces_kernel(parts_ref, out_ref):
    count = parts_ref.shape[0]
    total = parts_ref[0]
    for i in range(1, count):
        total = total + parts_ref[i]
    for i in range(count):
        out_ref[i] = total


def total_pieces(parts):
    return pl.pallas_call(
        pieces_kernel,
        out_shape=jax.ShapeDtypeStruct(parts.shape, F32),
        compiler_params=params(),
        name="total_pieces",
    )(parts)


def first_pass_kernel(*refs):
    grams, (s12_ref, s3_ref, basis_ref, inv_ref, gram_ref, a_ref, b_ref, slots) = refs[:-8], refs[-8:]
    sum_in_order(grams, slots, a_ref)
    invert_cholesky(a_ref, b_ref, inv_ref)
    basis = wide_turned(inv_ref[...], s12_ref[...], s12_ref[:RANK, :], s3_ref[...])
    basis_ref[...] = basis
    hi, mid, low = split3(basis)
    gram_ref[...] = square_nt(jnp.concatenate([hi, mid], axis=0), low)


def pass_scratch(count):
    return [pltpu.VMEM((RANK, RANK), F32)] * 2 + [pltpu.VMEM((count, RANK, RANK), F32)]


def pass_cost():
    return pl.CostEstimate(flops=4 * 10**9, bytes_accessed=2 * 10**7, transcendentals=0)


def first_pass(grams, s12, s3):
    square = jax.ShapeDtypeStruct((RANK, RANK), F32)
    return pl.pallas_call(
        first_pass_kernel,
        out_shape=[jax.ShapeDtypeStruct(s3.shape, F32), square, square],
        scratch_shapes=pass_scratch(len(grams)),
        compiler_params=params(),
        cost_estimate=pass_cost(),
        name="first_pass",
    )(*grams, s12, s3)


def second_pass_kernel(*refs):
    grams, (basis_one_ref, inv_one_ref, basis_ref, inv_ref, two_ref, a_ref, b_ref, slots) = refs[:-8], refs[-8:]
    sum_in_order(grams, slots, a_ref)
    invert_cholesky(a_ref, b_ref, two_ref)
    basis_ref[...] = wide_nt(basis_one_ref[...].T, two_ref[...])
    inv_ref[...] = mm32(two_ref[...], inv_one_ref[...])


def second_pass(grams, basis_one, inv_one):
    return pl.pallas_call(
        second_pass_kernel,
        out_shape=[
            jax.ShapeDtypeStruct(basis_one.shape[::-1], F32),
            jax.ShapeDtypeStruct(inv_one.shape, F32),
        ],
        scratch_shapes=[pltpu.VMEM((RANK, RANK), F32)] + pass_scratch(len(grams)),
        compiler_params=params(),
        cost_estimate=pass_cost(),
        name="second_pass",
    )(*grams, basis_one, inv_one)


def row_loads(g_hbm, e_hbm, g_ref, e_ref, sems, blocks):
    loads = []
    for k, (start, size) in enumerate(blocks):
        here, there = pl.ds(start - blocks[0][0], size), pl.ds(start, size)
        loads.append(pltpu.make_async_copy(g_hbm.at[there], g_ref.at[here], sems.at[2 * k]))
        loads.append(pltpu.make_async_copy(e_hbm.at[there], e_ref.at[here], sems.at[2 * k + 1]))
    return loads


def fetch_kernel(basis_ref, g_hbm, e_hbm, q3_ref, g_ref, e_ref, sems):
    loads = row_loads(g_hbm, e_hbm, g_ref, e_ref, sems, chunks_of(0, g_ref.shape[0], False))
    for load in loads:
        load.start()
    basis = basis_ref[...]
    hi = basis.astype(BF16)
    q3_ref[:, :RANK] = hi
    q3_ref[:, RANK : 2 * RANK] = (basis - hi.astype(F32)).astype(BF16)
    q3_ref[:, 2 * RANK :] = hi
    for load in loads:
        load.wait()


def fetch(basis, g, e, top):
    n, m = g.shape
    rows = jax.ShapeDtypeStruct((top, m), BF16)
    return pl.pallas_call(
        fetch_kernel,
        in_specs=[VMEM_SPEC, HBM_SPEC, HBM_SPEC],
        out_specs=[VMEM_SPEC] * 3,
        out_shape=[jax.ShapeDtypeStruct((n, 3 * RANK), BF16), rows, rows],
        scratch_shapes=[pltpu.SemaphoreType.DMA((2 * len(chunks_of(0, top, False)),))],
        compiler_params=params(FETCH_LIMIT),
        cost_estimate=pl.CostEstimate(flops=10**6, bytes_accessed=10**7, transcendentals=0),
        name="fetch",
    )(basis, g, e)


def residue_kernel(replicas, own_ref, other_ref, q3, inv_ref, g_top, e_top, g_hbm, e_hbm, right_hbm, new_hbm, halves, right3, right_ref, new_ref, g_ref, e_ref, in_sems, out_sems):
    core = lax.axis_index("core")
    count, piece = own_ref.shape[0], own_ref.shape[1]
    n, m = new_ref.shape
    top = g_top.shape[0]
    early, late = [(0, top)], chunks_of(top, n, True)
    loads = row_loads(g_hbm, e_hbm, g_ref, e_ref, in_sems, late)
    for load in loads:
        load.start()
    for i in range(count):
        halves[pl.ds(pl.multiple_of(core * (m // 2), 8) + i * piece, piece), :] = own_ref[i]
        halves[pl.ds(pl.multiple_of((1 - core) * (m // 2), 8) + i * piece, piece), :] = other_ref[i]
    right = wide_nt(halves[...], inv_ref[...]) * (1.0 / replicas)
    right_ref[...] = right
    right_copy = pltpu.make_async_copy(right_ref, right_hbm, out_sems.at[len(early) + len(late)])
    right_copy.start()
    hi = right.astype(BF16)
    right3[:, :RANK] = hi
    right3[:, RANK : 2 * RANK] = hi
    right3[:, 2 * RANK :] = (right - hi.astype(F32)).astype(BF16)
    copies = []
    for k, (first, size) in enumerate(early + late):
        rows = pl.ds(first, size)
        g_in, e_in, there = g_top, e_top, rows
        if first >= top:
            g_in, e_in, there = g_ref, e_ref, pl.ds(first - top, size)
            loads[2 * (k - len(early))].wait()
            loads[2 * (k - len(early)) + 1].wait()
        for start in range(0, m, COLS):
            cols = pl.ds(start, COLS)
            update = mm(q3[rows, :], right3[cols, :], NT)
            new_ref[rows, cols] = (g_in[there, cols].astype(F32) + e_in[there, cols].astype(F32) - update).astype(BF16)
        copies.append(pltpu.make_async_copy(new_ref.at[rows], new_hbm.at[rows], out_sems.at[k]))
        copies[-1].start()
    for copy in copies:
        copy.wait()
    right_copy.wait()


def residue(own, other, q3, inv, g_top, e_top, g, e, replicas):
    n, m = g.shape
    top = g_top.shape[0]
    early, late = [(0, top)], chunks_of(top, n, True)
    return pl.pallas_call(
        functools.partial(residue_kernel, replicas),
        in_specs=[VMEM_SPEC] * 6 + [HBM_SPEC] * 2,
        out_specs=[HBM_SPEC] * 2,
        out_shape=[jax.ShapeDtypeStruct((m, RANK), F32), jax.ShapeDtypeStruct((n, m), BF16)],
        scratch_shapes=[
            pltpu.VMEM((m, RANK), F32),
            pltpu.VMEM((m, 3 * RANK), BF16),
            pltpu.VMEM((m, RANK), F32),
            pltpu.VMEM((n, m), BF16),
            pltpu.VMEM((n - top, m), BF16),
            pltpu.VMEM((n - top, m), BF16),
            pltpu.SemaphoreType.DMA((2 * len(late),)),
            pltpu.SemaphoreType.DMA((len(early) + len(late) + 1,)),
        ],
        compiler_params=params(RESIDUE_LIMIT),
        name="residue",
    )(own, other, q3, inv, g_top, e_top, g, e)


def swap(x):
    return lax.ppermute(x, "core", [(0, 1), (1, 0)])


def round_fsdp(x, count):
    return [x] + [
        lax.ppermute(x, "fsdp", [(i, (i + k) % count) for i in range(count)]) for k in range(1, count)
    ]


def shards(gradients, errors, start_factor):
    g, e = gradients[0], errors[0]
    n = g.shape[0]
    ny, nx, nz = lax.axis_size("y"), lax.axis_size("fsdp"), lax.axis_size("tensor")
    keep, send = local_sketch(g, e, start_factor)
    pieces = (keep + swap(send)).reshape(ny * nz, -1, RANK)
    pieces = lax.all_to_all(pieces, ("y", "tensor"), 0, 0)
    own = lax.all_to_all(total_for_all(pieces), ("y", "tensor"), 0, 0).reshape(n // 2, RANK)
    s12, s3, gram = prepare(own, swap(own))
    grams = round_fsdp(gram, nx)
    got = swap(factor_send(s12, s3, g, e))
    parts = factor_keep(s12, s3, g, e, got).reshape(ny * nx, -1, RANK)
    parts = lax.all_to_all(parts, ("y", "fsdp"), 0, 0)
    basis_one, inv_one, gram = first_pass(grams, s12, s3)
    parts, _ = lax.optimization_barrier((parts, gram))
    grams = round_fsdp(gram, nx)
    own = lax.all_to_all(total_pieces(parts), ("y", "fsdp"), 0, 0)
    basis, inv = second_pass(grams, basis_one, inv_one)
    own, basis = lax.optimization_barrier((own, basis))
    other = swap(own)
    q3, g_top, e_top = fetch(basis, g, e, TOP)
    right_factor, new_errors = residue(own, other, q3, inv, g_top, e_top, g, e, 2 * ny)
    return (right_factor, new_errors[None])


def solution(mesh):
    shape = mesh.devices.shape
    split = Mesh(
        mesh.devices.reshape(shape[0] // 2, 2, *shape[1:]), ("y", "core", "fsdp", "tensor")
    )
    big = P(("y", "core"), "fsdp", "tensor")
    return jax.shard_map(
        shards,
        mesh=split,
        in_specs=(big, big, P("tensor", None)),
        out_specs=(P("tensor", None), big),
        check_vma=False,
    )
```

```python
import functools

import jax
import jax.numpy as jnp
from jax import lax
from jax.experimental import pallas as pl
from jax.experimental.pallas import tpu as pltpu
from jax.sharding import Mesh, PartitionSpec as P

F32, BF16 = jnp.float32, jnp.bfloat16
RANK = 128
ROWS = 256
COLS = 256
GROUP = 8
VMEM_LIMIT = 24 * 1024 * 1024
TOP = 384
FETCH_LIMIT = 51000000
RESIDUE_LIMIT = 51000000
STREAM_LIMIT = 55500000
NT = (((1,), (1,)), ((), ()))
NN = (((1,), (0,)), ((), ()))


def mm(a, b, dims=NN):
    return lax.dot_general(a, b, dims, preferred_element_type=F32)


def mm32(a, b, dims=NN):
    return lax.dot_general(a, b, dims, precision=lax.Precision.HIGHEST, preferred_element_type=F32)


def split3(x):
    hi = x.astype(BF16)
    rest = x - hi.astype(F32)
    mid = rest.astype(BF16)
    low = (rest - mid.astype(F32)).astype(BF16)
    return hi, mid, low


VMEM_SPEC = pl.BlockSpec(memory_space=pltpu.VMEM)
HBM_SPEC = pl.BlockSpec(memory_space=pltpu.HBM)


def params(limit=VMEM_LIMIT):
    return pltpu.CompilerParams(vmem_limit_bytes=limit)


def chunks_of(first, last, tail):
    blocks = []
    while first < last:
        size = min(ROWS, last - first)
        if tail and first + size == last and size == ROWS:
            size = ROWS // 2
        blocks.append((first, size))
        first += size
    return blocks


def sketch_kernel(g_hbm, e_hbm, p_hbm, keep_ref, send_ref, both_ref, p_ref, p12, p3, sems):
    n = g_hbm.shape[0]
    steps, ahead = n // ROWS, 2
    core = lax.axis_index("core")

    def load(i):
        rows = pl.ds(i * ROWS, ROWS)
        return (
            pltpu.make_async_copy(g_hbm.at[rows], both_ref.at[pl.ds(2 * i * ROWS, ROWS)], sems.at[2 * i]),
            pltpu.make_async_copy(e_hbm.at[rows], both_ref.at[pl.ds((2 * i + 1) * ROWS, ROWS)], sems.at[2 * i + 1]),
        )

    half = p_ref.shape[0] // 2
    halves = [pl.ds(0, half), pl.ds(half, half)]
    firsts = [
        pltpu.make_async_copy(p_hbm.at[rows], p_ref.at[rows], sems.at[2 * steps + k])
        for k, rows in enumerate(halves)
    ]
    for copy in firsts:
        copy.start()
    copies = [load(i) for i in range(steps)]
    for i in range(ahead):
        copies[i][0].start()
        copies[i][1].start()
    for copy, rows in zip(firsts, halves):
        copy.wait()
        hi, mid, low = split3(p_ref[rows, :])
        p12[rows, :RANK] = hi
        p12[rows, RANK:] = mid
        p3[rows, :] = low
    for i in range(steps):
        copies[i][0].wait()
        copies[i][1].wait()
        if i + ahead < steps:
            copies[i + ahead][0].start()
            copies[i + ahead][1].start()
        stacked = both_ref[pl.ds(2 * i * ROWS, 2 * ROWS), :]
        wide = mm(stacked, p12[...])
        wide = wide[:ROWS] + wide[ROWS:]
        block = wide[:, :RANK] + wide[:, RANK:] + mm(stacked[:ROWS] + stacked[ROWS:], p3[...])
        half = i // (steps // 2)
        place = pl.ds((i - half * (steps // 2)) * ROWS, ROWS)

        @pl.when(core == half)
        def _():
            keep_ref[place, :] = block

        @pl.when(core != half)
        def _():
            send_ref[place, :] = block


def local_sketch(g, e, p):
    n, m = g.shape
    half = jax.ShapeDtypeStruct((n // 2, RANK), F32)
    return pl.pallas_call(
        sketch_kernel,
        in_specs=[HBM_SPEC] * 3,
        out_specs=[VMEM_SPEC] * 2,
        out_shape=[half, half],
        scratch_shapes=[
            pltpu.VMEM((2 * n, m), BF16),
            pltpu.VMEM((m, RANK), F32),
            pltpu.VMEM((m, 2 * RANK), BF16),
            pltpu.VMEM((m, RANK), BF16),
            pltpu.SemaphoreType.DMA((2 * (n // ROWS) + 2,)),
        ],
        compiler_params=params(STREAM_LIMIT),
        name="local_sketch",
    )(g, e, p)


def total_kernel(parts_ref, out_ref):
    total = parts_ref[0]
    for i in range(1, parts_ref.shape[0]):
        total = total + parts_ref[i]
    for i in range(parts_ref.shape[0]):
        out_ref[i] = total


def total_for_all(parts):
    return pl.pallas_call(
        total_kernel,
        out_shape=jax.ShapeDtypeStruct(parts.shape, F32),
        compiler_params=params(),
        cost_estimate=pl.CostEstimate(flops=2 * 10**10, bytes_accessed=5 * 10**7, transcendentals=0),
        name="sketch_total",
    )(parts)


def tiles_of(width):
    return [(start, min(COLS, width - start)) for start in range(0, width, COLS)]


def factor_tile(s12_ref, s3_ref, g_ref, e_ref, side, width, start, size):
    cols = pl.ds(pl.multiple_of(side * width + start, RANK), size)
    g, e = g_ref[:, cols], e_ref[:, cols]
    both = mm(s12_ref[...], g) + mm(s12_ref[...], e)
    return (both[:RANK] + both[RANK:] + mm(s3_ref[...], g + e)).T


def wide_nt(x, w):
    x1, x2, x3 = split3(x)
    w1, w2, w3 = split3(w)
    front = jnp.concatenate(
        [jnp.concatenate([w1, w1], axis=1), jnp.concatenate([w2, w2], axis=1)], axis=0
    )
    both = mm(jnp.concatenate([x1, x2], axis=1), front, NT)
    rest = mm(jnp.concatenate([x1, x3], axis=1), jnp.concatenate([w3, w1], axis=1), NT)
    return both[:, :RANK] + (both[:, RANK:] + rest)


def wide_turned(w, x12, x1, x3):
    w1, w2, w3 = split3(w)
    front = jnp.concatenate(
        [jnp.concatenate([w1, w1], axis=1), jnp.concatenate([w2, w2], axis=1)], axis=0
    )
    both = mm(front, x12)
    rest = mm(w1, x3) + mm(w3, x1)
    return both[:RANK] + (both[RANK:] + rest)


def square_nt(hi_mid, low):
    square = mm(hi_mid, hi_mid, NT)
    cross = mm(hi_mid[:RANK], low, NT)
    return (
        square[:RANK, :RANK] + square[RANK:, RANK:]
        + (square[:RANK, RANK:] + square[RANK:, :RANK])
        + (cross + cross.T)
    )


def prepare_own_kernel(own_ref, o12_ref, o3_ref, gram_ref):
    hi, mid, low = split3(own_ref[...].T)
    o12_ref[:RANK, :] = hi
    o12_ref[RANK:, :] = mid
    o3_ref[...] = low
    gram_ref[...] = square_nt(o12_ref[...], low)


def prepare_own(own):
    half = own.shape[0]
    return pl.pallas_call(
        prepare_own_kernel,
        out_shape=[
            jax.ShapeDtypeStruct((2 * RANK, half), BF16),
            jax.ShapeDtypeStruct((RANK, half), BF16),
            jax.ShapeDtypeStruct((RANK, RANK), F32),
        ],
        compiler_params=params(),
        cost_estimate=pl.CostEstimate(flops=10**9, bytes_accessed=8 * 10**6, transcendentals=0),
        name="prepare_own",
    )(own)


def prepare_kernel(o12_ref, o3_ref, gram_own_ref, other_ref, s12_ref, s3_ref, gram_ref):
    core = lax.axis_index("core")
    half = other_ref.shape[0]
    mine = pl.ds(pl.multiple_of(core * half, half), half)
    theirs = pl.ds(pl.multiple_of((1 - core) * half, half), half)
    s12_ref[:, mine] = o12_ref[...]
    s3_ref[:, mine] = o3_ref[...]
    hi, mid, low = split3(other_ref[...].T)
    s12_ref[:RANK, theirs] = hi
    s12_ref[RANK:, theirs] = mid
    s3_ref[:, theirs] = low
    gram_ref[...] = gram_own_ref[...] + square_nt(jnp.concatenate([hi, mid], axis=0), low)


def prepare(o12, o3, gram_own, other):
    n = 2 * other.shape[0]
    return pl.pallas_call(
        prepare_kernel,
        out_shape=[
            jax.ShapeDtypeStruct((2 * RANK, n), BF16),
            jax.ShapeDtypeStruct((RANK, n), BF16),
            jax.ShapeDtypeStruct((RANK, RANK), F32),
        ],
        compiler_params=params(),
        name="prepare",
    )(o12, o3, gram_own, other)


def factor_send_kernel(s12_ref, s3_ref, g_ref, e_ref, send_ref):
    side, width = 1 - lax.axis_index("core"), send_ref.shape[0]
    for start, size in tiles_of(width):
        send_ref[start : start + size, :] = factor_tile(s12_ref, s3_ref, g_ref, e_ref, side, width, start, size)


def factor_keep_kernel(s12_ref, s3_ref, g_ref, e_ref, got_ref, out_hbm, sum_ref, sems):
    side, width = lax.axis_index("core"), got_ref.shape[0]
    copies = []
    for k, (start, size) in enumerate(tiles_of(width)):
        rows = pl.ds(start, size)
        sum_ref[rows, :] = got_ref[rows, :] + factor_tile(s12_ref, s3_ref, g_ref, e_ref, side, width, start, size)
        copies.append(pltpu.make_async_copy(sum_ref.at[rows], out_hbm.at[rows], sems.at[k]))
        copies[-1].start()
    for copy in copies:
        copy.wait()


def factor_cost():
    return pl.CostEstimate(flops=10**9, bytes_accessed=8 * 10**6, transcendentals=0)


def factor_send(s12, s3, g, e):
    return pl.pallas_call(
        factor_send_kernel,
        out_shape=jax.ShapeDtypeStruct((g.shape[1] // 2, RANK), F32),
        compiler_params=params(),
        cost_estimate=factor_cost(),
        name="factor_send",
    )(s12, s3, g, e)


def factor_keep(s12, s3, g, e, got):
    return pl.pallas_call(
        factor_keep_kernel,
        in_specs=[VMEM_SPEC] * 5,
        out_specs=HBM_SPEC,
        out_shape=jax.ShapeDtypeStruct(got.shape, F32),
        scratch_shapes=[
            pltpu.VMEM(got.shape, F32),
            pltpu.SemaphoreType.DMA((len(tiles_of(got.shape[0])),)),
        ],
        compiler_params=params(),
        cost_estimate=factor_cost(),
        name="factor_keep",
    )(s12, s3, g, e, got)


def sum_in_order(parts, slots, out_ref):
    count = len(parts)
    place = lax.axis_index("fsdp")
    for k in range(count):
        slots[lax.rem(place + count - k, count)] = parts[k][...]
    total = slots[0]
    for k in range(1, count):
        total = total + slots[k]
    out_ref[...] = total


def across(tile, lane):
    return jnp.broadcast_to(tile[:, lane : lane + 1], tile.shape)


def down(tile, row):
    return jnp.broadcast_to(tile[row : row + 1, :], tile.shape)


def tree_sum(terms):
    while len(terms) > 1:
        terms = [terms[i] + terms[i + 1] for i in range(0, len(terms), 2)]
    return terms[0]


def invert_cholesky(a_ref, b_ref, out_ref):
    tiles = RANK // 8
    lane = lax.broadcasted_iota(jnp.int32, (8, RANK), 1)
    row = lax.broadcasted_iota(jnp.int32, (8, RANK), 0)
    for t in range(tiles):
        b_ref[8 * t : 8 * t + 8, :] = jnp.where(lane == row + 8 * t, 1.0, 0.0)
    for first in range(0, RANK, GROUP):
        t, skip = first // 8, first % 8
        here = slice(8 * t, 8 * t + 8)
        a_tile, b_tile = a_ref[here, :], b_ref[here, :]
        columns = [across(a_tile, first + k) for k in range(GROUP)]
        value = {(i, k): down(columns[k], skip + i) for k in range(GROUP) for i in range(k, GROUP)}
        factor, inverse, root = {}, [], []
        for k in range(GROUP):
            inverse.append(1.0 / value[k, k])
            root.append(lax.rsqrt(value[k, k]))
            for i in range(k + 1, GROUP):
                factor[i, k] = value[i, k] * inverse[k]
            for j in range(k + 1, GROUP):
                for i in range(j, GROUP):
                    value[i, j] = value[i, j] - factor[j, k] * value[i, k]
        a_rows = [down(a_tile, skip + k) for k in range(GROUP)]
        b_rows = [down(b_tile, skip + k) for k in range(GROUP)]
        for k in range(GROUP):
            for i in range(k + 1, GROUP):
                a_rows[i] = a_rows[i] - factor[i, k] * a_rows[k]
                b_rows[i] = b_rows[i] - factor[i, k] * b_rows[k]
        for k in range(GROUP):
            out_ref[first + k : first + k + 1, :] = (b_rows[k] * root[k])[:1, :]
        a_rows = [a_rows[k] * inverse[k] for k in range(GROUP)]
        b_rows = [b_rows[k] * inverse[k] for k in range(GROUP)]
        for u in range(t if skip + GROUP < 8 else t + 1, tiles):
            there = slice(8 * u, 8 * u + 8)
            a_low, b_low = a_ref[there, :], b_ref[there, :]
            left = [across(a_low, first + k) for k in range(GROUP)]
            for k in range(GROUP):
                for i in range(k + 1, GROUP):
                    left[i] = left[i] - factor[i, k] * left[k]
            a_ref[there, :] = a_low - tree_sum([left[k] * a_rows[k] for k in range(GROUP)])
            b_ref[there, :] = b_low - tree_sum([left[k] * b_rows[k] for k in range(GROUP)])


def pieces_kernel(parts_ref, out_ref):
    count = parts_ref.shape[0]
    total = parts_ref[0]
    for i in range(1, count):
        total = total + parts_ref[i]
    for i in range(count):
        out_ref[i] = total


def total_pieces(parts):
    return pl.pallas_call(
        pieces_kernel,
        out_shape=jax.ShapeDtypeStruct(parts.shape, F32),
        compiler_params=params(),
        name="total_pieces",
    )(parts)


def first_pass_kernel(*refs):
    grams, (s12_ref, s3_ref, basis_ref, inv_ref, gram_ref, a_ref, b_ref, slots) = refs[:-8], refs[-8:]
    sum_in_order(grams, slots, a_ref)
    invert_cholesky(a_ref, b_ref, inv_ref)
    basis = wide_turned(inv_ref[...], s12_ref[...], s12_ref[:RANK, :], s3_ref[...])
    basis_ref[...] = basis
    hi, mid, low = split3(basis)
    gram_ref[...] = square_nt(jnp.concatenate([hi, mid], axis=0), low)


def pass_scratch(count):
    return [pltpu.VMEM((RANK, RANK), F32)] * 2 + [pltpu.VMEM((count, RANK, RANK), F32)]


def pass_cost():
    return pl.CostEstimate(flops=4 * 10**9, bytes_accessed=2 * 10**7, transcendentals=0)


def first_pass(grams, s12, s3):
    square = jax.ShapeDtypeStruct((RANK, RANK), F32)
    return pl.pallas_call(
        first_pass_kernel,
        out_shape=[jax.ShapeDtypeStruct(s3.shape, F32), square, square],
        scratch_shapes=pass_scratch(len(grams)),
        compiler_params=params(),
        cost_estimate=pass_cost(),
        name="first_pass",
    )(*grams, s12, s3)


def second_pass_kernel(*refs):
    grams, (basis_one_ref, inv_one_ref, basis_ref, inv_ref, two_ref, a_ref, b_ref, slots) = refs[:-8], refs[-8:]
    sum_in_order(grams, slots, a_ref)
    invert_cholesky(a_ref, b_ref, two_ref)
    basis_ref[...] = wide_nt(basis_one_ref[...].T, two_ref[...])
    inv_ref[...] = mm32(two_ref[...], inv_one_ref[...])


def second_pass(grams, basis_one, inv_one):
    return pl.pallas_call(
        second_pass_kernel,
        out_shape=[
            jax.ShapeDtypeStruct(basis_one.shape[::-1], F32),
            jax.ShapeDtypeStruct(inv_one.shape, F32),
        ],
        scratch_shapes=[pltpu.VMEM((RANK, RANK), F32)] + pass_scratch(len(grams)),
        compiler_params=params(),
        cost_estimate=pass_cost(),
        name="second_pass",
    )(*grams, basis_one, inv_one)


def row_loads(g_hbm, e_hbm, g_ref, e_ref, sems, blocks):
    loads = []
    for k, (start, size) in enumerate(blocks):
        here, there = pl.ds(start - blocks[0][0], size), pl.ds(start, size)
        loads.append(pltpu.make_async_copy(g_hbm.at[there], g_ref.at[here], sems.at[2 * k]))
        loads.append(pltpu.make_async_copy(e_hbm.at[there], e_ref.at[here], sems.at[2 * k + 1]))
    return loads


def fetch_kernel(basis_ref, g_hbm, e_hbm, q3_ref, g_ref, e_ref, sems):
    loads = row_loads(g_hbm, e_hbm, g_ref, e_ref, sems, chunks_of(0, g_ref.shape[0], False))
    for load in loads:
        load.start()
    basis = basis_ref[...]
    hi = basis.astype(BF16)
    q3_ref[:, :RANK] = hi
    q3_ref[:, RANK : 2 * RANK] = (basis - hi.astype(F32)).astype(BF16)
    q3_ref[:, 2 * RANK :] = hi
    for load in loads:
        load.wait()


def fetch(basis, g, e, top):
    n, m = g.shape
    rows = jax.ShapeDtypeStruct((top, m), BF16)
    return pl.pallas_call(
        fetch_kernel,
        in_specs=[VMEM_SPEC, HBM_SPEC, HBM_SPEC],
        out_specs=[VMEM_SPEC] * 3,
        out_shape=[jax.ShapeDtypeStruct((n, 3 * RANK), BF16), rows, rows],
        scratch_shapes=[pltpu.SemaphoreType.DMA((2 * len(chunks_of(0, top, False)),))],
        compiler_params=params(FETCH_LIMIT),
        cost_estimate=pl.CostEstimate(flops=10**6, bytes_accessed=10**7, transcendentals=0),
        name="fetch",
    )(basis, g, e)


def residue_kernel(replicas, own_ref, other_ref, q3, inv_ref, g_top, e_top, g_hbm, e_hbm, right_hbm, new_hbm, halves, right3, right_ref, new_ref, g_ref, e_ref, in_sems, out_sems):
    core = lax.axis_index("core")
    count, piece = own_ref.shape[0], own_ref.shape[1]
    n, m = new_ref.shape
    top = g_top.shape[0]
    early, late = [(0, top)], chunks_of(top, n, True)
    loads = row_loads(g_hbm, e_hbm, g_ref, e_ref, in_sems, late)
    for load in loads:
        load.start()
    for i in range(count):
        halves[pl.ds(pl.multiple_of(core * (m // 2), 8) + i * piece, piece), :] = own_ref[i]
        halves[pl.ds(pl.multiple_of((1 - core) * (m // 2), 8) + i * piece, piece), :] = other_ref[i]
    right = wide_nt(halves[...], inv_ref[...]) * (1.0 / replicas)
    right_ref[...] = right
    right_copy = pltpu.make_async_copy(right_ref, right_hbm, out_sems.at[len(early) + len(late)])
    right_copy.start()
    hi = right.astype(BF16)
    right3[:, :RANK] = hi
    right3[:, RANK : 2 * RANK] = hi
    right3[:, 2 * RANK :] = (right - hi.astype(F32)).astype(BF16)
    copies = []
    for k, (first, size) in enumerate(early + late):
        rows = pl.ds(first, size)
        g_in, e_in, there = g_top, e_top, rows
        if first >= top:
            g_in, e_in, there = g_ref, e_ref, pl.ds(first - top, size)
            loads[2 * (k - len(early))].wait()
            loads[2 * (k - len(early)) + 1].wait()
        for start in range(0, m, COLS):
            cols = pl.ds(start, COLS)
            update = mm(q3[rows, :], right3[cols, :], NT)
            new_ref[rows, cols] = (g_in[there, cols].astype(F32) + e_in[there, cols].astype(F32) - update).astype(BF16)
        copies.append(pltpu.make_async_copy(new_ref.at[rows], new_hbm.at[rows], out_sems.at[k]))
        copies[-1].start()
    for copy in copies:
        copy.wait()
    right_copy.wait()


def residue(own, other, q3, inv, g_top, e_top, g, e, replicas):
    n, m = g.shape
    top = g_top.shape[0]
    early, late = [(0, top)], chunks_of(top, n, True)
    return pl.pallas_call(
        functools.partial(residue_kernel, replicas),
        in_specs=[VMEM_SPEC] * 6 + [HBM_SPEC] * 2,
        out_specs=[HBM_SPEC] * 2,
        out_shape=[jax.ShapeDtypeStruct((m, RANK), F32), jax.ShapeDtypeStruct((n, m), BF16)],
        scratch_shapes=[
            pltpu.VMEM((m, RANK), F32),
            pltpu.VMEM((m, 3 * RANK), BF16),
            pltpu.VMEM((m, RANK), F32),
            pltpu.VMEM((n, m), BF16),
            pltpu.VMEM((n - top, m), BF16),
            pltpu.VMEM((n - top, m), BF16),
            pltpu.SemaphoreType.DMA((2 * len(late),)),
            pltpu.SemaphoreType.DMA((len(early) + len(late) + 1,)),
        ],
        compiler_params=params(RESIDUE_LIMIT),
        name="residue",
    )(own, other, q3, inv, g_top, e_top, g, e)


def swap(x):
    return lax.ppermute(x, "core", [(0, 1), (1, 0)])


def round_fsdp(x, count):
    return [x] + [
        lax.ppermute(x, "fsdp", [(i, (i + k) % count) for i in range(count)]) for k in range(1, count)
    ]


def shards(gradients, errors, start_factor):
    g, e = gradients[0], errors[0]
    n = g.shape[0]
    ny, nx, nz = lax.axis_size("y"), lax.axis_size("fsdp"), lax.axis_size("tensor")
    keep, send = local_sketch(g, e, start_factor)
    pieces = (keep + swap(send)).reshape(ny * nz, -1, RANK)
    pieces = lax.all_to_all(pieces, ("y", "tensor"), 0, 0)
    own = lax.all_to_all(total_for_all(pieces), ("y", "tensor"), 0, 0).reshape(n // 2, RANK)
    other = swap(own)
    s12, s3, gram = prepare(*prepare_own(own), other)
    grams = round_fsdp(gram, nx)
    got = swap(factor_send(s12, s3, g, e))
    parts = factor_keep(s12, s3, g, e, got).reshape(ny * nx, -1, RANK)
    parts = lax.all_to_all(parts, ("y", "fsdp"), 0, 0)
    basis_one, inv_one, gram = first_pass(grams, s12, s3)
    parts, _ = lax.optimization_barrier((parts, gram))
    grams = round_fsdp(gram, nx)
    own = lax.all_to_all(total_pieces(parts), ("y", "fsdp"), 0, 0)
    basis, inv = second_pass(grams, basis_one, inv_one)
    own, basis = lax.optimization_barrier((own, basis))
    other = swap(own)
    q3, g_top, e_top = fetch(basis, g, e, TOP)
    right_factor, new_errors = residue(own, other, q3, inv, g_top, e_top, g, e, 2 * ny)
    return (right_factor, new_errors[None])


def solution(mesh):
    shape = mesh.devices.shape
    split = Mesh(
        mesh.devices.reshape(shape[0] // 2, 2, *shape[1:]), ("y", "core", "fsdp", "tensor")
    )
    big = P(("y", "core"), "fsdp", "tensor")
    return jax.shard_map(
        shards,
        mesh=split,
        in_specs=(big, big, P("tensor", None)),
        out_specs=(P("tensor", None), big),
        check_vma=False,
    )
```
